32 devices in a mesh: grp: 2 (over y), row: 16 (over z, x, core).
Axes of the slice: x: 2, y: 2, z: 4, core: 2. Of those that a mesh axis runs over, the one named last changes fastest.
Arguments:
- points: bfloat16 [65536, 128], P(('grp', 'row')), as said below
- centers: bfloat16 [8192, 128], replicated, as said below
- inner_factor: bfloat16 [8192, 8192], P('row'), as said below
- outer_factor: bfloat16 [8192, 8192], P('row'), as said below
- iterate: float32 [64, 8192], P(None, 'row'), may hold values from -6 to 6
- residual: float32 [64, 8192], P(None, 'row'), as said below
- direction: float32 [64, 8192], P(None, 'row'), as said below
Outputs:
- next_iterate: float32 [64, 8192], P(None, 'row')
- next_residual: float32 [64, 8192], P(None, 'row')
- next_direction: float32 [64, 8192], P(None, 'row')
The draws below stay inside these ranges and needn't reach their ends.
Inputs may be any that keep to these rules, and one draw needn't show every extreme that they name: `inner_factor`: upper triangular: zero below the diagonal, positive on it. `outer_factor`: upper triangular: zero below the diagonal, positive on it. `residual`: finite real values. `direction`: finite real values. `points`: finite real values. `centers`: finite real values.
All inputs are finite; a program needn't handle non-finite values.
Results may differ from the reference program's by a relative error of at most 0.0056.
Values may be sent and summed in bfloat16 or wider, within the bound.
A program may use at most 64 MiB of HBM per device.

```python
import math
import jax
import jax.numpy as jnp
from jax import lax

D = 128
M = 8192
R = 64
N_DEV = 2048
NPTS = 65536


def upper_factor(key, lowest, highest, spread):
    key_diag, key_off = jax.random.split(key)
    position = jnp.arange(M)
    above = position[None, :] > position[:, None]
    on_diag = position[None, :] == position[:, None]
    off_values = jax.random.uniform(key_off, (M, M), jnp.float32, -1.0, 1.0) * (spread * math.sqrt(3.0 / M))
    diag_values = jnp.exp(jax.random.uniform(key_diag, (M,), jnp.float32, math.log(lowest), math.log(highest)))
    filled = jnp.where(above, off_values, 0.0)
    return jnp.where(on_diag, diag_values[:, None], filled)


def draw_inner_factor(key, part):
    return upper_factor(jax.random.fold_in(key, 11), 1.0, 3.0, 1.0).astype(jnp.bfloat16)


def draw_outer_factor(key, part):
    return upper_factor(jax.random.fold_in(key, 12), 100.0, 400.0, 120.0).astype(jnp.bfloat16)


def point_cloud(key):
    key_center, key_noise, key_owner, key_scale, key_shift = jax.random.split(jax.random.fold_in(key, 31), 5)
    center_values = jnp.clip(jax.random.normal(key_center, (M, D), jnp.float32), -6.0, 6.0)
    shift_values = jnp.clip(jax.random.normal(key_shift, (M, D), jnp.float32), -6.0, 6.0) * 0.2
    device_count = NPTS // N_DEV
    span = max(M * N_DEV // NPTS, 1)
    index = jnp.arange(NPTS, dtype=jnp.int32)
    device = index // N_DEV
    local_owner = jax.random.randint(key_owner, (NPTS,), 0, span, dtype=jnp.int32)
    owner = (device * M // device_count + local_owner).astype(jnp.int32)
    point_scale = jnp.exp(jax.random.uniform(key_scale, (NPTS, 1), jnp.float32, math.log(0.05), math.log(0.7)))
    noise = jnp.clip(jax.random.normal(key_noise, (NPTS, D), jnp.float32), -6.0, 6.0) * point_scale
    point_values = center_values[owner] + shift_values[owner] + noise
    return (center_values, point_values)


def draw_centers(key, part):
    return point_cloud(key)[0].astype(jnp.bfloat16)


def draw_points(key, part):
    return point_cloud(key)[1].astype(jnp.bfloat16)


def scaled_state(key):
    key_base, key_row, key_col = jax.random.split(key, 3)
    position = jnp.arange(M).astype(jnp.float32) / max(M - 1, 1)
    base = jax.random.normal(key_base, (R, M), jnp.float32)
    row_scale = jnp.exp(jax.random.uniform(key_row, (M,), jnp.float32, math.log(0.3), math.log(3.0)))
    ramp = 1.0 + (math.sqrt(3.0) - 1.0) * position
    col_scale = jnp.exp(jax.random.uniform(key_col, (R,), jnp.float32, math.log(0.3), math.log(3.0)))
    return base * (row_scale * ramp)[None, :] * col_scale[:, None]


def draw_residual(key, part):
    return scaled_state(jax.random.fold_in(key, 21)).astype(jnp.float32)


def draw_direction(key, part):
    return scaled_state(jax.random.fold_in(key, 22)).astype(jnp.float32)


def shard_levels(key, dims, cuts, low, largest):
    def one(dim, shards_of):
        heights = jax.random.uniform(jax.random.fold_in(jax.random.fold_in(key, 6), dim), (shards_of,), jnp.float32, low / len(cuts), largest / len(cuts))
        return jnp.repeat(jnp.exp(heights), dims[dim] // shards_of).reshape((-1,) + (1,) * (len(dims) - dim - 1))

    gain = one(*cuts[0])
    for cut in cuts[1:]:
        gain = gain * one(*cut)
    return gain


def gaussian(stream_key, dims, scale, reach, cuts=(), held_as=jnp.bfloat16):
    drawn = scale * jax.random.normal(stream_key, dims, jnp.float32)
    if cuts:
        drawn = drawn * shard_levels(stream_key, dims, cuts, -0.22, 0.18)
    return jnp.clip(drawn, -reach, reach).astype(held_as)


def setup_inputs(seed: int = 0) -> dict:
    key_of = jax.random.split(jax.random.key(seed), 8)
    return {
        "points": draw_points(jax.random.fold_in(key_of[7], 71), 0),
        "centers": draw_centers(jax.random.fold_in(key_of[7], 71), 0),
        "inner_factor": draw_inner_factor(jax.random.fold_in(key_of[7], 71), 0),
        "outer_factor": draw_outer_factor(jax.random.fold_in(key_of[7], 71), 0),
        "iterate": gaussian(key_of[4], (R, M), 1.0, 6.0, ((1, 16),), jnp.float32),
        "residual": draw_residual(jax.random.fold_in(key_of[7], 71), 0),
        "direction": draw_direction(jax.random.fold_in(key_of[7], 71), 0),
    }


ridge_weight = 0.5


def kernel_rows(block_points, centers, center_norms):
    point_wide = block_points.astype(jnp.float32)
    point_norms = jnp.sum(point_wide * point_wide, axis=1)
    cross_term = lax.dot_general(block_points, centers, (((1,), (1,)), ((), ())), preferred_element_type=jnp.float32)
    distance = point_norms[:, None] + center_norms[None, :] - 2.0 * cross_term
    return jnp.exp(distance * (-4.0 / D)).astype(jnp.bfloat16)


def reference(points, centers, inner_factor, outer_factor, iterate, residual, direction):
    contract_last = (((1,), (1,)), ((), ()))
    direction_half = direction.astype(jnp.bfloat16)
    inner_term = lax.dot_general(direction_half, inner_factor, contract_last, preferred_element_type=jnp.float32)
    inner_half = inner_term.astype(jnp.bfloat16)
    outer_half = lax.dot_general(inner_half, outer_factor, contract_last, preferred_element_type=jnp.float32).astype(jnp.bfloat16)
    center_wide = centers.astype(jnp.float32)
    center_norms = jnp.sum(center_wide * center_wide, axis=1)
    block_rows = math.gcd(NPTS, 4096)
    point_blocks = points.reshape(NPTS // block_rows, block_rows, D)

    def one_block(carried, block_points):
        kernel_block = kernel_rows(block_points, centers, center_norms)
        fitted = lax.dot_general(outer_half, kernel_block, contract_last, preferred_element_type=jnp.float32).astype(jnp.bfloat16)
        return carried + jnp.dot(fitted, kernel_block, preferred_element_type=jnp.float32), None

    normal_eq, _ = lax.scan(one_block, jnp.zeros((R, M), jnp.float32), point_blocks)
    normal_half = normal_eq.astype(jnp.bfloat16)
    shaped = jnp.dot(normal_half, outer_factor, preferred_element_type=jnp.float32) / NPTS + ridge_weight * inner_term
    shaped_half = shaped.astype(jnp.bfloat16)
    operator_image = jnp.dot(shaped_half, inner_factor, preferred_element_type=jnp.float32)
    old_norm = jnp.sum(residual * residual, axis=1)
    curvature = jnp.sum(direction * operator_image, axis=1)
    step_size = (old_norm / curvature)[:, None]
    next_iterate = iterate + step_size * direction
    next_residual = residual - step_size * operator_image
    new_norm = jnp.sum(next_residual * next_residual, axis=1)
    next_direction = next_residual + (new_norm / old_norm)[:, None] * direction
    return (next_iterate, next_residual, next_direction)
```

```python
import functools
import math

import jax
import jax.numpy as jnp
from jax import lax
from jax.experimental import pallas as pl
from jax.experimental.pallas import tpu as pltpu
from jax.sharding import PartitionSpec as P

ridge_weight = 0.5
MESH = pl.DeviceIdType.MESH
LAST = (((1,), (1,)), ((), ()))
f32, bf16 = jnp.float32, jnp.bfloat16

A1, A1S, A2, A2S, A3, A3S, A3Y, A3O, NC, NY, NP, O_S, O_P, I_S, I_P, CHANNELS = range(16)
Y1, Y2, YN, YS, YI, SINGLES = range(6)


def nt(a, b):
    return lax.dot_general(a, b, LAST, preferred_element_type=f32)


def mm(a, b):
    return jnp.dot(a, b, preferred_element_type=f32)


def norm_columns(wide, first, other):
    scale = 4.0 / wide.shape[1]
    norms = jnp.minimum(jnp.sum(wide * wide, axis=1, keepdims=True), 3e38) * -scale
    high = norms.astype(bf16).astype(f32)
    mid = (norms - high).astype(bf16).astype(f32)
    low = norms - high - mid
    lane = lax.broadcasted_iota(jnp.int32, wide.shape, 1)
    held = jnp.where(lane == first, high, 0.0)
    held = jnp.where(lane == first + 1, mid, held)
    held = jnp.where(lane == first + 2, low, held)
    held = jnp.where((lane >= other) & (lane < other + 3), 1.0, held)
    return held.astype(bf16)


def kernel(
    groups, n, point_count,
    points_hbm, centers_hbm, inner_hbm, outer_hbm, iterate, residual, direction,
    next_iterate, next_residual, next_direction,
    gram, inner_v, outer_v, points_v, centers_v, points_aug, centers_aug,
    half1, half2, own3, oth3, fit, fit_half, acc, ytx1, yrx1, ytx2, yrx2, inner_term,
    ctx, keep, ys, tx, nc_rx, ny_rx, np_rx, os_rx, op_rx, is_rx, ip_rx,
    normal_half, shaped_half, image, pair_sums, dots,
    lsem, ssem, rsem, ssing, rsing, psend, precv, dsend, drecv,
):
    pairs = n // 2
    own = inner_hbm.shape[0]
    targets = direction.shape[0]
    dims = points_hbm.shape[1]
    g, r = lax.axis_index("grp"), lax.axis_index("row")
    q, c, p = lax.rem(g, 2), lax.rem(r, 2), r // 2
    base = g - q
    active = c == q
    idle = c != q
    sib = (g, r + 1 - 2 * c)
    across = (g + 1 - 2 * q, r)

    def peer(k):
        return (g, 2 * k + q)

    def rc(src, dst, ch, si, ri, dev):
        return pltpu.make_async_remote_copy(
            src_ref=src, dst_ref=dst, send_sem=ssem.at[ch, si], recv_sem=rsem.at[ch, ri],
            device_id=dev, device_id_type=MESH)

    def single(src, dst, ch):
        return pltpu.make_async_remote_copy(
            src_ref=src, dst_ref=dst, send_sem=ssing.at[ch], recv_sem=rsing.at[ch],
            device_id=across, device_id_type=MESH)

    def loop(lo, hi, body):
        def step(s, carry):
            body(s)
            return carry
        lax.fori_loop(lo, hi, step, 0)

    def back(s):
        return lax.rem(p - s + 2 * pairs, pairs)

    def ahead(s):
        return lax.rem(p + 1 + s, pairs)

    points_in = pltpu.make_async_copy(points_hbm, points_v, lsem.at[2, 0])
    centers_in = pltpu.make_async_copy(centers_hbm, centers_v, lsem.at[2, 1])
    points_in.start()
    centers_in.start()

    def slab(factor, held, which, k):
        columns = pl.ds(pl.multiple_of((2 * k + q) * own, own), own)
        return pltpu.make_async_copy(factor.at[:, columns], held.at[k], lsem.at[which, k])

    loop(0, pairs, lambda s: slab(inner_hbm, inner_v, 0, back(s)).start())
    loop(0, pairs, lambda s: slab(outer_hbm, outer_v, 1, back(s)).start())

    @pl.when(active)
    def _():
        half1[p] = direction[...].astype(bf16)

    barrier = pltpu.get_barrier_semaphore()

    def greet(d):
        gg, rr = base + d // n, lax.rem(d, n)

        @pl.when((gg != g) | (rr != r))
        def _():
            pl.semaphore_signal(barrier, inc=1, device_id=(gg, rr), device_id_type=MESH)

    loop(0, 2 * n, greet)
    for h in range(groups // 2 if groups > 2 else 0):
        @pl.when(2 * h + q != g)
        def _():
            pl.semaphore_signal(barrier, inc=1, device_id=(2 * h + q, r), device_id_type=MESH)
    pl.semaphore_wait(barrier, 2 * n - 1 + groups // 2 - 1)

    def spread(half, ch):
        @pl.when(active)
        def _():
            loop(1, pairs, lambda s: rc(
                half.at[p], half.at[p], ch, lax.rem(p + s, pairs), p, peer(lax.rem(p + s, pairs))).start())
            rc(half.at[p], half.at[p], ch + 1, p, p, sib).start()

    def take(half, ch, s, k):
        @pl.when(active & (s > 0))
        def _():
            rc(half.at[k], half.at[k], ch, k, k, sib).wait_recv()
            rc(half.at[k], half.at[k], ch + 1, k, k, sib).start()

        @pl.when(idle)
        def _():
            rc(half.at[k], half.at[k], ch + 1, k, k, sib).wait_recv()

    tile = min(512, points_hbm.shape[0])

    def gram_block(b):
        rows = pl.ds(pl.multiple_of(b * own, own), own)
        block = centers_v[rows, :]
        centers_aug[:, :dims] = block
        centers_aug[:, dims:] = norm_columns(block.astype(f32), 3, 0)
        for i in range(points_hbm.shape[0] // tile):
            at = slice(i * tile, (i + 1) * tile)
            power = nt(points_aug[at, :], centers_aug[...])
            gram[b, at, :] = jnp.exp2(power * math.log2(math.e)).astype(bf16)

    spread(half1, A1)
    points_in.wait()
    for i in range(points_hbm.shape[0] // tile):
        at = slice(i * tile, (i + 1) * tile)
        block = points_v[at, :]
        wide = block.astype(f32)
        points_aug[at, :dims] = (wide * (8.0 / dims)).astype(bf16)
        points_aug[at, dims:] = norm_columns(wide, 0, 3)
    centers_in.wait()

    acc[...] = jnp.zeros_like(acc)

    def inner_step(s):
        k = back(s)
        take(half1, A1, s, k)
        slab(inner_hbm, inner_v, 0, k).wait()
        acc[...] += nt(half1[k], inner_v[k])
        gram_block(s)

    loop(0, pairs, inner_step)

    @pl.when(idle)
    def _():
        ytx1[...] = acc[...]
        single(ytx1, yrx1, Y1).start()

    @pl.when(active)
    def _():
        single(ytx1, yrx1, Y1).wait_recv()
        total = acc[...] + yrx1[...]
        inner_term[...] = total
        half2[p] = total.astype(bf16)

    spread(half2, A2)
    acc[...] = jnp.zeros_like(acc)

    def outer_step(s):
        k = back(s)
        take(half2, A2, s, k)
        slab(outer_hbm, outer_v, 1, k).wait()
        acc[...] += nt(half2[k], outer_v[k])
        gram_block(pairs + s)

    loop(0, pairs, outer_step)

    @pl.when(idle)
    def _():
        ytx2[...] = acc[...]
        single(ytx2, yrx2, Y2).start()

    @pl.when(active)
    def _():
        single(ytx2, yrx2, Y2).wait_recv()
        own3[p] = (acc[...] + yrx2[...]).astype(bf16)
        rc(own3.at[p], oth3.at[p], A3Y, p, p, across).start()

    spread(own3, A3)
    fit[...] = jnp.zeros_like(fit)

    def fit_step(s):
        k, k1, k2 = back(s), back(s - 1), back(s - 2)

        @pl.when(s < pairs)
        def _():
            take(own3, A3, s, k)

            @pl.when(active & (s > 0))
            def _():
                rc(own3.at[k], oth3.at[k], A3Y, k, k, across).start()

        @pl.when(idle & (s > 0) & (s <= pairs))
        def _():
            rc(oth3.at[k1], oth3.at[k1], A3Y, k1, k1, across).wait_recv()
            rc(oth3.at[k1], oth3.at[k1], A3O, k1, k1, sib).start()

        @pl.when(s < pairs)
        def _():
            fit[...] += nt(own3[k], gram[2 * k + q])

        @pl.when(s >= 2)
        def _():
            @pl.when(active)
            def _():
                rc(oth3.at[k2], oth3.at[k2], A3O, k2, k2, sib).wait_recv()

            fit[...] += nt(oth3[k2], gram[2 * k2 + 1 - q])

    loop(0, pairs + 2, fit_step)
    fit_half[...] = fit[...].astype(bf16)

    def normal_step(s):
        k, k1, k2 = ahead(s), ahead(s - 1 + pairs), ahead(s - 2 + pairs)

        @pl.when(s < pairs)
        def _():
            ctx[k] = mm(fit_half[...], gram[2 * k + 1 - c]).astype(bf16)
            rc(ctx.at[k], nc_rx.at[k], NC, k, k, sib).start()
            keep[k] = mm(fit_half[...], gram[2 * k + c])

        @pl.when((s >= 1) & (s <= pairs))
        def _():
            rc(ctx.at[k1], nc_rx.at[k1], NC, k1, k1, sib).wait_recv()
            total = keep[k1] + nc_rx[k1].astype(f32)

            @pl.when(idle)
            def _():
                ys[k1] = total.astype(bf16)
                rc(ys.at[k1], ny_rx.at[k1], NY, k1, k1, across).start()

            @pl.when(active)
            def _():
                keep[k1] = total

        @pl.when(active & (s >= 2))
        def _():
            rc(ys.at[k2], ny_rx.at[k2], NY, k2, k2, across).wait_recv()
            deliver(keep[k2] + ny_rx[k2].astype(f32), k2, np_rx, NP)

    def deliver(total, k, rx, ch):
        @pl.when(k != p)
        def _():
            tx[k] = total.astype(bf16)
            rc(tx.at[k], rx.at[p], ch, k, p, peer(k)).start()

        @pl.when(k == p)
        def _():
            keep[k] = total

    def collect(rx, ch):
        acc[...] = keep[p]

        def one(s):
            k = back(s)
            rc(tx.at[k], rx.at[k], ch, k, k, sib).wait_recv()
            acc[...] += rx[k].astype(f32)

        loop(1, pairs, one)

    def sent(src, ch, with_own):
        def one(k):
            if with_own:
                rc(src.at[k], src.at[k], ch, k, k, sib).wait_send()
            else:
                @pl.when(k != p)
                def _():
                    rc(src.at[k], src.at[k], ch, k, k, sib).wait_send()
        loop(0, pairs, one)

    loop(0, pairs + 2, normal_step)
    sent(ctx, NC, True)

    @pl.when(active)
    def _():
        collect(np_rx, NP)
        if groups > 2:
            mine = g // 2
            pair_sums[mine] = acc[...]

            def pair_copy(h, to):
                return pltpu.make_async_remote_copy(
                    src_ref=pair_sums.at[h], dst_ref=pair_sums.at[h], send_sem=psend.at[to],
                    recv_sem=precv.at[h], device_id=(2 * to + q, r), device_id_type=MESH)

            for h in range(groups // 2):
                @pl.when(h != mine)
                def _():
                    pair_copy(mine, h).start()
            for h in range(groups // 2):
                @pl.when(h != mine)
                def _():
                    pair_copy(h, h).wait_recv()
            total = pair_sums[0]
            for h in range(1, groups // 2):
                total = total + pair_sums[h]
            acc[...] = total
            for h in range(groups // 2):
                @pl.when(h != mine)
                def _():
                    pair_copy(mine, h).wait_send()
        normal_half[...] = acc[...].astype(bf16)
        single(normal_half, normal_half, YN).start()
        sent(tx, NP, False)

    @pl.when(idle)
    def _():
        single(normal_half, normal_half, YN).wait_recv()

    def transposed(held, lhs, s_rx, p_rx, ch_s, ch_p):
        def one(s):
            k, k1 = ahead(s), ahead(s - 1 + pairs)

            @pl.when(s < pairs)
            def _():
                term = mm(lhs[...], held[k])

                @pl.when(idle)
                def _():
                    ctx[k] = term.astype(bf16)
                    rc(ctx.at[k], s_rx.at[k], ch_s, k, k, sib).start()

                @pl.when(active)
                def _():
                    keep[k] = term

            @pl.when(active & (s >= 1))
            def _():
                rc(ctx.at[k1], s_rx.at[k1], ch_s, k1, k1, sib).wait_recv()
                deliver(keep[k1] + s_rx[k1].astype(f32), k1, p_rx, ch_p)

        loop(0, pairs + 1, one)

        @pl.when(active)
        def _():
            collect(p_rx, ch_p)
            sent(tx, ch_p, False)

        @pl.when(idle)
        def _():
            sent(ctx, ch_s, True)

    transposed(outer_v, normal_half, os_rx, op_rx, O_S, O_P)

    @pl.when(active)
    def _():
        shaped = acc[...] * (1.0 / point_count) + ridge_weight * inner_term[...]
        shaped_half[...] = shaped.astype(bf16)
        single(shaped_half, shaped_half, YS).start()

    @pl.when(idle)
    def _():
        single(shaped_half, shaped_half, YS).wait_recv()

    transposed(inner_v, shaped_half, is_rx, ip_rx, I_S, I_P)

    def dot_copy(slot, d):
        return pltpu.make_async_remote_copy(
            src_ref=dots.at[slot], dst_ref=dots.at[slot], send_sem=dsend.at[d], recv_sem=drecv.at[slot],
            device_id=(base + d // n, lax.rem(d, n)), device_id_type=MESH)

    me = q * n + r
    lane = lax.broadcasted_iota(jnp.int32, (targets, 128), 1)

    @pl.when(active)
    def _():
        image[...] = acc[...]
        x, y, z = acc[...], residual[...], direction[...]
        packed = jnp.zeros((targets, 128), f32)
        for at, pair in enumerate(((y, y), (z, x), (y, x), (x, x))):
            packed = jnp.where(lane == at, jnp.sum(pair[0] * pair[1], axis=1, keepdims=True), packed)
        square = jnp.concatenate([packed, jnp.zeros((128 - targets, 128), f32)], axis=0)
        dots[r] = square.T[:8, :]

        def one(d):
            @pl.when(d != me)
            def _():
                dot_copy(r, d).start()

        loop(0, 2 * n, one)
        single(image, image, YI).start()

    def arrived(slot):
        @pl.when(idle | (slot != r))
        def _():
            dot_copy(slot, me).wait_recv()

    loop(0, n, arrived)
    totals = dots[0]
    for slot in range(1, n):
        totals = totals + dots[slot]
    square = jnp.concatenate([totals, jnp.zeros((120, 128), f32)], axis=0).T

    @pl.when(idle)
    def _():
        single(image, image, YI).wait_recv()

    old_norm, curvature = square[:targets, 0:1], square[:targets, 1:2]
    cross_sum, image_norm = square[:targets, 2:3], square[:targets, 3:4]
    step_size = old_norm / curvature
    new_norm = old_norm - 2.0 * step_size * cross_sum + step_size * step_size * image_norm
    following = residual[...] - step_size * image[...]
    next_residual[...] = following
    next_iterate[...] = iterate[...] + step_size * direction[...]
    next_direction[...] = following + (new_norm / old_norm) * direction[...]

    @pl.when(active)
    def _():
        sent(half1, A1, False)
        sent(half1, A1S, True)
        sent(half2, A2, False)
        sent(half2, A2S, True)
        sent(own3, A3, False)
        sent(own3, A3S, True)
        sent(own3, A3Y, True)
        single(normal_half, normal_half, YN).wait_send()
        single(shaped_half, shaped_half, YS).wait_send()
        single(image, image, YI).wait_send()

        def one(d):
            @pl.when(d != me)
            def _():
                dot_copy(r, d).wait_send()

        loop(0, 2 * n, one)

    @pl.when(idle)
    def _():
        single(ytx1, yrx1, Y1).wait_send()
        single(ytx2, yrx2, Y2).wait_send()
        sent(oth3, A3O, True)
        sent(ys, NY, True)


def local(groups, n, points, centers, inner_factor, outer_factor, iterate, residual, direction):
    pairs, own = n // 2, inner_factor.shape[0]
    count, dims = points.shape
    targets = direction.shape[0]
    half = pltpu.VMEM((pairs, targets, own), bf16)
    block = pltpu.VMEM((targets, own), f32)
    slabs = pltpu.VMEM((pairs, own, own), bf16)
    vmem = pl.BlockSpec(memory_space=pltpu.VMEM)
    anywhere = pl.BlockSpec(memory_space=pl.ANY)
    dma = pltpu.SemaphoreType.DMA
    return tuple(pl.pallas_call(
        functools.partial(kernel, groups, n, count * groups * n),
        out_shape=[jax.ShapeDtypeStruct((targets, own), f32)] * 3,
        in_specs=[anywhere] * 4 + [vmem] * 3,
        out_specs=[vmem] * 3,
        scratch_shapes=[
            pltpu.VMEM((n, count, own), bf16), slabs, slabs,
            pltpu.VMEM((count, dims), bf16), pltpu.VMEM(centers.shape, bf16),
            pltpu.VMEM((count, 2 * dims), bf16), pltpu.VMEM((own, 2 * dims), bf16),
            half, half, half, half,
            pltpu.VMEM((targets, count), f32), pltpu.VMEM((targets, count), bf16),
            block, block, block, block, block, block,
            half, pltpu.VMEM((pairs, targets, own), f32), half, half,
            half, half, half, half, half, half, half,
            pltpu.VMEM((targets, own), bf16), pltpu.VMEM((targets, own), bf16), block,
            pltpu.VMEM((max(groups // 2, 1), targets, own) if groups > 2 else (1, 8, 128), f32),
            pltpu.VMEM((n, 8, 128), f32),
            dma((3, max(pairs, 2))), dma((CHANNELS, pairs)), dma((CHANNELS, pairs)),
            dma((SINGLES,)), dma((SINGLES,)),
            dma((max(groups // 2, 1),)), dma((max(groups // 2, 1),)), dma((2 * n,)), dma((n,)),
        ],
        compiler_params=pltpu.CompilerParams(
            collective_id=0, has_side_effects=True, vmem_limit_bytes=60 * 1024 * 1024
        ),
        cost_estimate=pl.CostEstimate(
            flops=2 * count * centers.shape[0] * (dims + 2 * targets),
            bytes_accessed=4 * own * centers.shape[0], transcendentals=count * centers.shape[0]),
    )(points, centers, inner_factor, outer_factor, iterate, residual, direction))


def solution(mesh):
    placed = (
        P(("grp", "row"), None), P(), P("row", None), P("row", None),
        P(None, "row"), P(None, "row"), P(None, "row"),
    )
    return jax.shard_map(
        functools.partial(local, mesh.shape["grp"], mesh.shape["row"]),
        mesh=mesh,
        in_specs=placed,
        out_specs=(P(None, "row"), P(None, "row"), P(None, "row")),
        check_vma=False,
    )
```

```python
import functools

import jax
import jax.numpy as jnp
from jax import lax
from jax.experimental import pallas as pl
from jax.experimental.pallas import tpu as pltpu
from jax.sharding import PartitionSpec as P

ridge_weight = 0.5
MESH = pl.DeviceIdType.MESH
LAST = (((1,), (1,)), ((), ()))
f32, bf16 = jnp.float32, jnp.bfloat16

A1, A1S, A2, A2S, A3, A3S, A3Y, A3O, NC, NY, NP, O_S, O_P, I_S, I_P, CHANNELS = range(16)
Y1, Y2, YN, YS, YI, SINGLES = range(6)


def nt(a, b):
    return lax.dot_general(a, b, LAST, preferred_element_type=f32)


def mm(a, b):
    return jnp.dot(a, b, preferred_element_type=f32)


def norm_columns(wide, first, other):
    scale = 4.0 / wide.shape[1]
    norms = jnp.minimum(jnp.sum(wide * wide, axis=1, keepdims=True), 3e38) * -scale
    high = norms.astype(bf16).astype(f32)
    mid = (norms - high).astype(bf16).astype(f32)
    low = norms - high - mid
    lane = lax.broadcasted_iota(jnp.int32, wide.shape, 1)
    held = jnp.where(lane == first, high, 0.0)
    held = jnp.where(lane == first + 1, mid, held)
    held = jnp.where(lane == first + 2, low, held)
    held = jnp.where((lane >= other) & (lane < other + 3), 1.0, held)
    return held


def kernel(
    groups, n, point_count,
    points_hbm, centers_hbm, inner_hbm, outer_hbm, residual, direction, image, factors,
    gram, inner_v, outer_v, points_v, centers_v, points_aug, centers_aug,
    half1, half2, own3, oth3, fit, fit_half, acc, ytx1, yrx1, ytx2, yrx2, inner_term,
    ctx, keep, ys, tx, nc_rx, ny_rx, np_rx, os_rx, op_rx, is_rx, ip_rx,
    normal_half, shaped_half, pair_sums, dots,
    lsem, ssem, rsem, ssing, rsing, psend, precv, dsend, drecv,
):
    pairs = n // 2
    own = inner_hbm.shape[0]
    targets = direction.shape[0]
    dims = points_hbm.shape[1]
    g, r = lax.axis_index("grp"), lax.axis_index("row")
    q, c, p = lax.rem(g, 2), lax.rem(r, 2), r // 2
    base = g - q
    active = c == q
    idle = c != q
    sib = (g, r + 1 - 2 * c)
    across = (g + 1 - 2 * q, r)

    def peer(k):
        return (g, 2 * k + q)

    def rc(src, dst, ch, si, ri, dev):
        return pltpu.make_async_remote_copy(
            src_ref=src, dst_ref=dst, send_sem=ssem.at[ch, si], recv_sem=rsem.at[ch, ri],
            device_id=dev, device_id_type=MESH)

    def single(src, dst, ch):
        return pltpu.make_async_remote_copy(
            src_ref=src, dst_ref=dst, send_sem=ssing.at[ch], recv_sem=rsing.at[ch],
            device_id=across, device_id_type=MESH)

    def loop(lo, hi, body):
        def step(s, carry):
            body(s)
            return carry
        lax.fori_loop(lo, hi, step, 0)

    def back(s):
        return lax.rem(p - s + 2 * pairs, pairs)

    def ahead(s):
        return lax.rem(p + 1 + s, pairs)

    points_in = pltpu.make_async_copy(points_hbm, points_v, lsem.at[2, 0])
    centers_in = pltpu.make_async_copy(centers_hbm, centers_v, lsem.at[2, 1])
    points_in.start()
    centers_in.start()

    def slab(factor, held, which, k):
        columns = pl.ds(pl.multiple_of((2 * k + q) * own, own), own)
        return pltpu.make_async_copy(factor.at[:, columns], held.at[k], lsem.at[which, k])

    loop(0, pairs, lambda s: slab(inner_hbm, inner_v, 0, back(s)).start())
    loop(0, pairs, lambda s: slab(outer_hbm, outer_v, 1, back(s)).start())

    @pl.when(active)
    def _():
        half1[p] = direction[...].astype(bf16)

    barrier = pltpu.get_barrier_semaphore()

    def greet(d):
        gg, rr = base + d // n, lax.rem(d, n)

        @pl.when((gg != g) | (rr != r))
        def _():
            pl.semaphore_signal(barrier, inc=1, device_id=(gg, rr), device_id_type=MESH)

    loop(0, 2 * n, greet)
    for h in range(groups // 2 if groups > 2 else 0):
        @pl.when(2 * h + q != g)
        def _():
            pl.semaphore_signal(barrier, inc=1, device_id=(2 * h + q, r), device_id_type=MESH)
    pl.semaphore_wait(barrier, 2 * n - 1 + groups // 2 - 1)

    def spread(half, ch):
        @pl.when(active)
        def _():
            loop(1, pairs, lambda s: rc(
                half.at[p], half.at[p], ch, lax.rem(p + s, pairs), p, peer(lax.rem(p + s, pairs))).start())
            rc(half.at[p], half.at[p], ch + 1, p, p, sib).start()

    def take(half, ch, s, k):
        @pl.when(active & (s > 0))
        def _():
            rc(half.at[k], half.at[k], ch, k, k, sib).wait_recv()
            rc(half.at[k], half.at[k], ch + 1, k, k, sib).start()

        @pl.when(idle)
        def _():
            rc(half.at[k], half.at[k], ch + 1, k, k, sib).wait_recv()

    tile = min(512, points_hbm.shape[0])

    def gram_block(b):
        rows = pl.ds(pl.multiple_of(b * own, own), own)
        block = centers_v[rows, :]
        wide = block.astype(f32)
        centers_aug[:dims, :] = wide.T.astype(bf16)
        centers_aug[dims:, :] = norm_columns(wide, 3, 0).T.astype(bf16)
        for i in range(points_hbm.shape[0] // tile):
            at = slice(i * tile, (i + 1) * tile)
            gram[b, at, :] = jnp.exp(mm(points_aug[at, :], centers_aug[...])).astype(bf16)

    spread(half1, A1)
    points_in.wait()
    for i in range(points_hbm.shape[0] // tile):
        at = slice(i * tile, (i + 1) * tile)
        block = points_v[at, :]
        wide = block.astype(f32)
        points_aug[at, :dims] = (wide * (8.0 / dims)).astype(bf16)
        points_aug[at, dims:] = norm_columns(wide, 0, 3).astype(bf16)
    centers_in.wait()

    acc[...] = jnp.zeros_like(acc)

    def inner_step(s):
        k = back(s)
        take(half1, A1, s, k)
        slab(inner_hbm, inner_v, 0, k).wait()
        acc[...] += nt(half1[k], inner_v[k])
        gram_block(s)

    loop(0, pairs, inner_step)

    @pl.when(idle)
    def _():
        ytx1[...] = acc[...]
        single(ytx1, yrx1, Y1).start()

    @pl.when(active)
    def _():
        single(ytx1, yrx1, Y1).wait_recv()
        total = acc[...] + yrx1[...]
        inner_term[...] = total
        half2[p] = total.astype(bf16)

    spread(half2, A2)
    acc[...] = jnp.zeros_like(acc)

    def outer_step(s):
        k = back(s)
        take(half2, A2, s, k)
        slab(outer_hbm, outer_v, 1, k).wait()
        acc[...] += nt(half2[k], outer_v[k])
        gram_block(pairs + s)

    loop(0, pairs, outer_step)

    @pl.when(idle)
    def _():
        ytx2[...] = acc[...]
        single(ytx2, yrx2, Y2).start()

    @pl.when(active)
    def _():
        single(ytx2, yrx2, Y2).wait_recv()
        own3[p] = (acc[...] + yrx2[...]).astype(bf16)
        rc(own3.at[p], oth3.at[p], A3Y, p, p, across).start()

    spread(own3, A3)
    fit[...] = jnp.zeros_like(fit)

    def fit_step(s):
        k, k1, k2 = back(s), back(s - 1), back(s - 2)

        @pl.when(s < pairs)
        def _():
            take(own3, A3, s, k)

            @pl.when(active & (s > 0))
            def _():
                rc(own3.at[k], oth3.at[k], A3Y, k, k, across).start()

        @pl.when(idle & (s > 0) & (s <= pairs))
        def _():
            rc(oth3.at[k1], oth3.at[k1], A3Y, k1, k1, across).wait_recv()
            rc(oth3.at[k1], oth3.at[k1], A3O, k1, k1, sib).start()

        @pl.when(s < pairs)
        def _():
            fit[...] += nt(own3[k], gram[2 * k + q])

        @pl.when(s >= 2)
        def _():
            @pl.when(active)
            def _():
                rc(oth3.at[k2], oth3.at[k2], A3O, k2, k2, sib).wait_recv()

            fit[...] += nt(oth3[k2], gram[2 * k2 + 1 - q])

    loop(0, pairs + 2, fit_step)
    fit_half[...] = fit[...].astype(bf16)

    def normal_step(s):
        k, k1, k2 = ahead(s), ahead(s - 1 + pairs), ahead(s - 2 + pairs)

        @pl.when(s < pairs)
        def _():
            ctx[k] = mm(fit_half[...], gram[2 * k + 1 - c]).astype(bf16)
            rc(ctx.at[k], nc_rx.at[k], NC, k, k, sib).start()
            keep[k] = mm(fit_half[...], gram[2 * k + c])

        @pl.when((s >= 1) & (s <= pairs))
        def _():
            rc(ctx.at[k1], nc_rx.at[k1], NC, k1, k1, sib).wait_recv()
            total = keep[k1] + nc_rx[k1].astype(f32)

            @pl.when(idle)
            def _():
                ys[k1] = total.astype(bf16)
                rc(ys.at[k1], ny_rx.at[k1], NY, k1, k1, across).start()

            @pl.when(active)
            def _():
                keep[k1] = total

        @pl.when(active & (s >= 2))
        def _():
            rc(ys.at[k2], ny_rx.at[k2], NY, k2, k2, across).wait_recv()
            deliver(keep[k2] + ny_rx[k2].astype(f32), k2, np_rx, NP)

    def deliver(total, k, rx, ch):
        @pl.when(k != p)
        def _():
            tx[k] = total.astype(bf16)
            rc(tx.at[k], rx.at[p], ch, k, p, peer(k)).start()

        @pl.when(k == p)
        def _():
            keep[k] = total

    def collect(rx, ch):
        acc[...] = keep[p]

        def one(s):
            k = back(s)
            rc(tx.at[k], rx.at[k], ch, k, k, sib).wait_recv()
            acc[...] += rx[k].astype(f32)

        loop(1, pairs, one)

    def sent(src, ch, with_own):
        def one(k):
            if with_own:
                rc(src.at[k], src.at[k], ch, k, k, sib).wait_send()
            else:
                @pl.when(k != p)
                def _():
                    rc(src.at[k], src.at[k], ch, k, k, sib).wait_send()
        loop(0, pairs, one)

    loop(0, pairs + 2, normal_step)
    sent(ctx, NC, True)

    @pl.when(active)
    def _():
        collect(np_rx, NP)
        if groups > 2:
            mine = g // 2
            pair_sums[mine] = acc[...]

            def pair_copy(h, to):
                return pltpu.make_async_remote_copy(
                    src_ref=pair_sums.at[h], dst_ref=pair_sums.at[h], send_sem=psend.at[to],
                    recv_sem=precv.at[h], device_id=(2 * to + q, r), device_id_type=MESH)

            for h in range(groups // 2):
                @pl.when(h != mine)
                def _():
                    pair_copy(mine, h).start()
            for h in range(groups // 2):
                @pl.when(h != mine)
                def _():
                    pair_copy(h, h).wait_recv()
            total = pair_sums[0]
            for h in range(1, groups // 2):
                total = total + pair_sums[h]
            acc[...] = total
            for h in range(groups // 2):
                @pl.when(h != mine)
                def _():
                    pair_copy(mine, h).wait_send()
        normal_half[...] = acc[...].astype(bf16)
        single(normal_half, normal_half, YN).start()
        sent(tx, NP, False)

    @pl.when(idle)
    def _():
        single(normal_half, normal_half, YN).wait_recv()

    def transposed(held, lhs, s_rx, p_rx, ch_s, ch_p):
        def one(s):
            k, k1 = ahead(s), ahead(s - 1 + pairs)

            @pl.when(s < pairs)
            def _():
                term = mm(lhs[...], held[k])

                @pl.when(idle)
                def _():
                    ctx[k] = term.astype(bf16)
                    rc(ctx.at[k], s_rx.at[k], ch_s, k, k, sib).start()

                @pl.when(active)
                def _():
                    keep[k] = term

            @pl.when(active & (s >= 1))
            def _():
                rc(ctx.at[k1], s_rx.at[k1], ch_s, k1, k1, sib).wait_recv()
                deliver(keep[k1] + s_rx[k1].astype(f32), k1, p_rx, ch_p)

        loop(0, pairs + 1, one)

        @pl.when(active)
        def _():
            collect(p_rx, ch_p)
            sent(tx, ch_p, False)

        @pl.when(idle)
        def _():
            sent(ctx, ch_s, True)

    transposed(outer_v, normal_half, os_rx, op_rx, O_S, O_P)

    @pl.when(active)
    def _():
        shaped = acc[...] * (1.0 / point_count) + ridge_weight * inner_term[...]
        shaped_half[...] = shaped.astype(bf16)
        single(shaped_half, shaped_half, YS).start()

    @pl.when(idle)
    def _():
        single(shaped_half, shaped_half, YS).wait_recv()

    transposed(inner_v, shaped_half, is_rx, ip_rx, I_S, I_P)

    def dot_copy(slot, d):
        return pltpu.make_async_remote_copy(
            src_ref=dots.at[slot], dst_ref=dots.at[slot], send_sem=dsend.at[d], recv_sem=drecv.at[slot],
            device_id=(base + d // n, lax.rem(d, n)), device_id_type=MESH)

    me = q * n + r
    lane = lax.broadcasted_iota(jnp.int32, (targets, 128), 1)

    @pl.when(active)
    def _():
        image[...] = acc[...]
        x, y, z = acc[...], residual[...], direction[...]
        packed = jnp.zeros((targets, 128), f32)
        for at, pair in enumerate(((y, y), (z, x), (y, x), (x, x))):
            packed = jnp.where(lane == at, jnp.sum(pair[0] * pair[1], axis=1, keepdims=True), packed)
        square = jnp.concatenate([packed, jnp.zeros((128 - targets, 128), f32)], axis=0)
        dots[r] = square.T[:8, :]

        def one(d):
            @pl.when(d != me)
            def _():
                dot_copy(r, d).start()

        loop(0, 2 * n, one)
        single(image, image, YI).start()

    def arrived(slot):
        @pl.when(idle | (slot != r))
        def _():
            dot_copy(slot, me).wait_recv()

    loop(0, n, arrived)
    totals = dots[0]
    for slot in range(1, n):
        totals = totals + dots[slot]
    square = jnp.concatenate([totals, jnp.zeros((120, 128), f32)], axis=0).T

    @pl.when(idle)
    def _():
        single(image, image, YI).wait_recv()

    old_norm, curvature = square[:targets, 0:1], square[:targets, 1:2]
    cross_sum, image_norm = square[:targets, 2:3], square[:targets, 3:4]
    step_size = old_norm / curvature
    new_norm = old_norm - 2.0 * step_size * cross_sum + step_size * step_size * image_norm
    factors[...] = jnp.where(lane == 0, step_size, new_norm / old_norm)

    @pl.when(active)
    def _():
        sent(half1, A1, False)
        sent(half1, A1S, True)
        sent(half2, A2, False)
        sent(half2, A2S, True)
        sent(own3, A3, False)
        sent(own3, A3S, True)
        sent(own3, A3Y, True)
        single(normal_half, normal_half, YN).wait_send()
        single(shaped_half, shaped_half, YS).wait_send()
        single(image, image, YI).wait_send()

        def one(d):
            @pl.when(d != me)
            def _():
                dot_copy(r, d).wait_send()

        loop(0, 2 * n, one)

    @pl.when(idle)
    def _():
        single(ytx1, yrx1, Y1).wait_send()
        single(ytx2, yrx2, Y2).wait_send()
        sent(oth3, A3O, True)
        sent(ys, NY, True)


def update(image, factors, iterate, residual, direction, next_iterate, next_residual, next_direction):
    step_size, ratio = factors[:, 0:1], factors[:, 1:2]
    following = residual[...] - step_size * image[...]
    next_residual[...] = following
    next_iterate[...] = iterate[...] + step_size * direction[...]
    next_direction[...] = following + ratio * direction[...]


def local(groups, n, points, centers, inner_factor, outer_factor, iterate, residual, direction):
    pairs, own = n // 2, inner_factor.shape[0]
    count, dims = points.shape
    targets = direction.shape[0]
    half = pltpu.VMEM((pairs, targets, own), bf16)
    block = pltpu.VMEM((targets, own), f32)
    slabs = pltpu.VMEM((pairs, own, own), bf16)
    vmem = pl.BlockSpec(memory_space=pltpu.VMEM)
    anywhere = pl.BlockSpec(memory_space=pl.ANY)
    dma = pltpu.SemaphoreType.DMA
    image, factors = pl.pallas_call(
        functools.partial(kernel, groups, n, count * groups * n),
        out_shape=[jax.ShapeDtypeStruct((targets, own), f32), jax.ShapeDtypeStruct((targets, 128), f32)],
        in_specs=[anywhere] * 4 + [vmem] * 2,
        out_specs=[vmem] * 2,
        scratch_shapes=[
            pltpu.VMEM((n, count, own), bf16), slabs, slabs,
            pltpu.VMEM((count, dims), bf16), pltpu.VMEM(centers.shape, bf16),
            pltpu.VMEM((count, 2 * dims), bf16), pltpu.VMEM((2 * dims, own), bf16),
            half, half, half, half,
            pltpu.VMEM((targets, count), f32), pltpu.VMEM((targets, count), bf16),
            block, block, block, block, block, block,
            half, pltpu.VMEM((pairs, targets, own), f32), half, half,
            half, half, half, half, half, half, half,
            pltpu.VMEM((targets, own), bf16), pltpu.VMEM((targets, own), bf16),
            pltpu.VMEM((max(groups // 2, 1), targets, own) if groups > 2 else (1, 8, 128), f32),
            pltpu.VMEM((n, 8, 128), f32),
            dma((3, max(pairs, 2))), dma((CHANNELS, pairs)), dma((CHANNELS, pairs)),
            dma((SINGLES,)), dma((SINGLES,)),
            dma((max(groups // 2, 1),)), dma((max(groups // 2, 1),)), dma((2 * n,)), dma((n,)),
        ],
        compiler_params=pltpu.CompilerParams(
            collective_id=0, has_side_effects=True, vmem_limit_bytes=60 * 1024 * 1024
        ),
        cost_estimate=pl.CostEstimate(
            flops=2 * count * centers.shape[0] * (dims + 2 * targets),
            bytes_accessed=4 * own * centers.shape[0], transcendentals=count * centers.shape[0]),
    )(points, centers, inner_factor, outer_factor, residual, direction)
    return tuple(pl.pallas_call(
        update,
        out_shape=[jax.ShapeDtypeStruct((targets, own), f32)] * 3,
        in_specs=[vmem] * 5,
        out_specs=[vmem] * 3,
    )(image, factors, iterate, residual, direction))


def solution(mesh):
    placed = (
        P(("grp", "row"), None), P(), P("row", None), P("row", None),
        P(None, "row"), P(None, "row"), P(None, "row"),
    )
    return jax.shard_map(
        functools.partial(local, mesh.shape["grp"], mesh.shape["row"]),
        mesh=mesh,
        in_specs=placed,
        out_specs=(P(None, "row"), P(None, "row"), P(None, "row")),
        check_vma=False,
    )
```

```python
import functools

import jax
import jax.numpy as jnp
from jax import lax
from jax.experimental import pallas as pl
from jax.experimental.pallas import tpu as pltpu
from jax.sharding import PartitionSpec as P

ridge_weight = 0.5
MESH = pl.DeviceIdType.MESH
LAST = (((1,), (1,)), ((), ()))
f32, bf16 = jnp.float32, jnp.bfloat16

A1, A1M, A2, A2M, A3, A3M, A3S, NC, NY, NP, O_M, O_P, I_M, I_P, CHANNELS = range(15)


def nt(a, b):
    return lax.dot_general(a, b, LAST, preferred_element_type=f32)


def mm(a, b):
    return jnp.dot(a, b, preferred_element_type=f32)


def norm_columns(wide, first, other):
    scale = 4.0 / wide.shape[1]
    norms = jnp.minimum(jnp.sum(wide * wide, axis=1, keepdims=True), 3e38) * -scale
    high = norms.astype(bf16).astype(f32)
    mid = (norms - high).astype(bf16).astype(f32)
    low = norms - high - mid
    lane = lax.broadcasted_iota(jnp.int32, wide.shape, 1)
    held = jnp.where(lane == first, high, 0.0)
    held = jnp.where(lane == first + 1, mid, held)
    held = jnp.where(lane == first + 2, low, held)
    held = jnp.where((lane >= other) & (lane < other + 3), 1.0, held)
    return held


def kernel(
    groups, n, point_count,
    points_hbm, centers_hbm, inner_hbm, outer_hbm, residual, direction, image, factors,
    gram, inner_v, outer_v, points_v, centers_v, points_aug, centers_aug,
    half1, half2, half3, fit, fit_half, acc, inner_term,
    ctx, keep, tx, nc_rx, ny_rx, np_rx, om_rx, op_rx, im_rx, ip_rx,
    normal_half, shaped_half, pair_sums, dots,
    lsem, csem, ssem, rsem, isem, psend, precv, dsend, drecv,
):
    pairs = n // 2
    own = inner_hbm.shape[0]
    targets = direction.shape[0]
    dims = points_hbm.shape[1]
    g, r = lax.axis_index("grp"), lax.axis_index("row")
    q, c, p = lax.rem(g, 2), lax.rem(r, 2), r // 2
    base = g - q
    active = c == q
    idle = c != q
    sib = (g, r + 1 - 2 * c)
    across = (g + 1 - 2 * q, r)
    mate = (g + 1 - 2 * q, r + 1 - 2 * c)

    def peer(k):
        return (g, 2 * k + q)

    def rc(src, dst, ch, si, ri, dev):
        return pltpu.make_async_remote_copy(
            src_ref=src, dst_ref=dst, send_sem=ssem.at[ch, si], recv_sem=rsem.at[ch, ri],
            device_id=dev, device_id_type=MESH)

    def loop(lo, hi, body):
        def step(s, carry):
            body(s)
            return carry
        lax.fori_loop(lo, hi, step, 0)

    def back(s):
        return lax.rem(p - s + 2 * pairs, pairs)

    def ahead(s):
        return lax.rem(p + 1 + s, pairs)

    points_in = pltpu.make_async_copy(points_hbm, points_v, csem.at[2])
    points_in.start()

    def center_copy(b):
        slot = lax.rem(b, 2)
        rows = pl.ds(pl.multiple_of(b * own, own), own)
        return pltpu.make_async_copy(centers_hbm.at[rows, :], centers_v.at[slot], csem.at[slot])

    center_copy(0).start()

    def slab(factor, held, which, b):
        columns = pl.ds(pl.multiple_of(b * own, own), own)
        return pltpu.make_async_copy(factor.at[:, columns], held.at[b], lsem.at[which, b])

    @pl.when(active)
    def _():
        def load(factor, held, which):
            def one(s):
                slab(factor, held, which, 2 * back(s) + q).start()
                slab(factor, held, which, 2 * back(s) + 1 - q).start()
            loop(0, pairs, one)

        load(inner_hbm, inner_v, 0)
        load(outer_hbm, outer_v, 1)
        half1[r] = direction[...].astype(bf16)

    barrier = pltpu.get_barrier_semaphore()

    def greet(d):
        gg, rr = base + d // n, lax.rem(d, n)

        @pl.when((gg != g) | (rr != r))
        def _():
            pl.semaphore_signal(barrier, inc=1, device_id=(gg, rr), device_id_type=MESH)

    loop(0, 2 * n, greet)
    for h in range(groups // 2 if groups > 2 else 0):
        @pl.when(2 * h + q != g)
        def _():
            pl.semaphore_signal(barrier, inc=1, device_id=(2 * h + q, r), device_id_type=MESH)
    pl.semaphore_wait(barrier, 2 * n - 1 + groups // 2 - 1)

    def spread(half, ch):
        loop(1, pairs, lambda s: rc(
            half.at[r], half.at[r], ch, lax.rem(p + s, pairs), p, peer(lax.rem(p + s, pairs))).start())
        rc(half.at[r], half.at[r], ch + 1, p, p, mate).start()

    def take_own(half, ch, s):
        b = 2 * back(s) + q

        @pl.when(s > 0)
        def _():
            rc(half.at[b], half.at[b], ch, back(s), back(s), mate).wait_recv()
            rc(half.at[b], half.at[b], ch + 1, back(s), back(s), mate).start()

    def take_other(half, ch, s):
        b = 2 * back(s) + 1 - q
        rc(half.at[b], half.at[b], ch + 1, back(s), back(s), mate).wait_recv()

    tile = min(512, points_hbm.shape[0])

    def gram_block(b):
        @pl.when(b + 1 < n)
        def _():
            center_copy(b + 1).start()

        center_copy(b).wait()
        wide = centers_v[lax.rem(b, 2)].astype(f32)
        centers_aug[:dims, :] = wide.T.astype(bf16)
        centers_aug[dims:, :] = norm_columns(wide, 3, 0).T.astype(bf16)
        for i in range(points_hbm.shape[0] // tile):
            at = slice(i * tile, (i + 1) * tile)
            gram[b, at, :] = jnp.exp(mm(points_aug[at, :], centers_aug[...])).astype(bf16)

    @pl.when(active)
    def _():
        spread(half1, A1)

    points_in.wait()
    for i in range(points_hbm.shape[0] // tile):
        at = slice(i * tile, (i + 1) * tile)
        block = points_v[at, :]
        wide = block.astype(f32)
        points_aug[at, :dims] = (wide * (8.0 / dims)).astype(bf16)
        points_aug[at, dims:] = norm_columns(wide, 0, 3).astype(bf16)

    def product(half, held, which, ch, first):
        acc[...] = jnp.zeros_like(acc)

        def one(s):
            @pl.when(active & (s < pairs))
            def _():
                take_own(half, ch, s)
                b = 2 * back(s) + q
                slab(inner_hbm, held, which, b).wait()
                acc[...] += nt(half[b], held[b])

            @pl.when(active & (s >= 2))
            def _():
                take_other(half, ch, s - 2)
                b = 2 * back(s - 2) + 1 - q
                slab(inner_hbm, held, which, b).wait()
                acc[...] += nt(half[b], held[b])

            @pl.when(s < pairs)
            def _():
                gram_block(first + s)

        loop(0, pairs + 2, one)

    product(half1, inner_v, 0, A1, 0)

    @pl.when(active)
    def _():
        inner_term[...] = acc[...]
        half2[r] = acc[...].astype(bf16)
        spread(half2, A2)

    product(half2, outer_v, 1, A2, pairs)

    @pl.when(active)
    def _():
        half3[r] = acc[...].astype(bf16)
        spread(half3, A3)

    fit[...] = jnp.zeros_like(fit)

    def fit_step(s):
        def chip(b):
            copy = rc(half3.at[b], half3.at[b], A3S, b, b, sib)

            @pl.when(active)
            def _():
                copy.start()

            @pl.when(idle)
            def _():
                copy.wait_recv()

            fit[...] += nt(half3[b], gram[b])

        @pl.when(s < pairs)
        def _():
            @pl.when(active)
            def _():
                take_own(half3, A3, s)

            chip(2 * back(s) + q)

        @pl.when(s >= 2)
        def _():
            @pl.when(active)
            def _():
                take_other(half3, A3, s - 2)

            chip(2 * back(s - 2) + 1 - q)

    loop(0, pairs + 2, fit_step)
    fit_half[...] = fit[...].astype(bf16)

    def normal_step(s):
        k, k1, k2 = ahead(s), ahead(s - 1 + pairs), ahead(s - 2 + pairs)

        @pl.when(s < pairs)
        def _():
            ctx[k] = mm(fit_half[...], gram[2 * k + 1 - c]).astype(bf16)
            rc(ctx.at[k], nc_rx.at[k], NC, k, k, sib).start()
            keep[k] = mm(fit_half[...], gram[2 * k + c])

        @pl.when((s >= 1) & (s <= pairs))
        def _():
            rc(ctx.at[k1], nc_rx.at[k1], NC, k1, k1, sib).wait_recv()
            total = keep[k1] + nc_rx[k1].astype(f32)

            @pl.when(idle)
            def _():
                tx[k1] = total.astype(bf16)
                rc(tx.at[k1], ny_rx.at[k1], NY, k1, k1, across).start()

            @pl.when(active)
            def _():
                keep[k1] = total

        @pl.when(active & (s >= 2))
        def _():
            rc(tx.at[k2], ny_rx.at[k2], NY, k2, k2, across).wait_recv()
            deliver(keep[k2] + ny_rx[k2].astype(f32), k2, np_rx, NP)

    def deliver(total, k, rx, ch):
        @pl.when(k != p)
        def _():
            tx[k] = total.astype(bf16)
            rc(tx.at[k], rx.at[p], ch, k, p, peer(k)).start()

        @pl.when(k == p)
        def _():
            keep[k] = total

    def collect(rx, ch):
        acc[...] = keep[p]

        def one(s):
            k = back(s)
            rc(tx.at[k], rx.at[k], ch, k, k, sib).wait_recv()
            acc[...] += rx[k].astype(f32)

        loop(1, pairs, one)

    def sent(src, ch, with_own):
        def one(k):
            if with_own:
                rc(src.at[k], src.at[k], ch, k, k, sib).wait_send()
            else:
                @pl.when(k != p)
                def _():
                    rc(src.at[k], src.at[k], ch, k, k, sib).wait_send()
        loop(0, pairs, one)

    loop(0, pairs + 2, normal_step)
    sent(ctx, NC, True)

    @pl.when(active)
    def _():
        collect(np_rx, NP)
        if groups > 2:
            mine = g // 2
            pair_sums[mine] = acc[...]

            def pair_copy(h, to):
                return pltpu.make_async_remote_copy(
                    src_ref=pair_sums.at[h], dst_ref=pair_sums.at[h], send_sem=psend.at[to],
                    recv_sem=precv.at[h], device_id=(2 * to + q, r), device_id_type=MESH)

            for h in range(groups // 2):
                @pl.when(h != mine)
                def _():
                    pair_copy(mine, h).start()
            for h in range(groups // 2):
                @pl.when(h != mine)
                def _():
                    pair_copy(h, h).wait_recv()
            total = pair_sums[0]
            for h in range(1, groups // 2):
                total = total + pair_sums[h]
            acc[...] = total
            for h in range(groups // 2):
                @pl.when(h != mine)
                def _():
                    pair_copy(mine, h).wait_send()
        sent(tx, NP, False)
        normal_half[...] = acc[...].astype(bf16)

    def transposed(held, lhs, m_rx, p_rx, ch_m, ch_p):
        def one(s):
            k, k1 = ahead(s), ahead(s - 1 + pairs)

            @pl.when(s < pairs)
            def _():
                ctx[k] = mm(lhs[...], held[2 * k + 1 - q]).astype(bf16)
                rc(ctx.at[k], m_rx.at[k], ch_m, k, k, mate).start()
                keep[k] = mm(lhs[...], held[2 * k + q])

            @pl.when(s >= 1)
            def _():
                rc(ctx.at[k1], m_rx.at[k1], ch_m, k1, k1, mate).wait_recv()
                deliver(keep[k1] + m_rx[k1].astype(f32), k1, p_rx, ch_p)

        loop(0, pairs + 1, one)
        collect(p_rx, ch_p)
        sent(tx, ch_p, False)
        sent(ctx, ch_m, True)

    @pl.when(active)
    def _():
        transposed(outer_v, normal_half, om_rx, op_rx, O_M, O_P)
        shaped = acc[...] * (1.0 / point_count) + ridge_weight * inner_term[...]
        shaped_half[...] = shaped.astype(bf16)
        transposed(inner_v, shaped_half, im_rx, ip_rx, I_M, I_P)

    def dot_copy(slot, d):
        return pltpu.make_async_remote_copy(
            src_ref=dots.at[slot], dst_ref=dots.at[slot], send_sem=dsend.at[d], recv_sem=drecv.at[slot],
            device_id=(base + d // n, lax.rem(d, n)), device_id_type=MESH)

    image_copy = pltpu.make_async_remote_copy(
        src_ref=image, dst_ref=image, send_sem=isem.at[0], recv_sem=isem.at[1], device_id=across, device_id_type=MESH)
    me = q * n + r
    lane = lax.broadcasted_iota(jnp.int32, (targets, 128), 1)

    @pl.when(active)
    def _():
        image[...] = acc[...]
        x, y, z = acc[...], residual[...], direction[...]
        packed = jnp.zeros((targets, 128), f32)
        for at, pair in enumerate(((y, y), (z, x), (y, x), (x, x))):
            packed = jnp.where(lane == at, jnp.sum(pair[0] * pair[1], axis=1, keepdims=True), packed)
        square = jnp.concatenate([packed, jnp.zeros((128 - targets, 128), f32)], axis=0)
        dots[r] = square.T[:8, :]

        def one(d):
            @pl.when(d != me)
            def _():
                dot_copy(r, d).start()

        loop(0, 2 * n, one)
        image_copy.start()

    def arrived(slot):
        @pl.when(idle | (slot != r))
        def _():
            dot_copy(slot, me).wait_recv()

    loop(0, n, arrived)
    totals = dots[0]
    for slot in range(1, n):
        totals = totals + dots[slot]
    square = jnp.concatenate([totals, jnp.zeros((120, 128), f32)], axis=0).T

    @pl.when(idle)
    def _():
        image_copy.wait_recv()

    old_norm, curvature = square[:targets, 0:1], square[:targets, 1:2]
    cross_sum, image_norm = square[:targets, 2:3], square[:targets, 3:4]
    step_size = old_norm / curvature
    new_norm = old_norm - 2.0 * step_size * cross_sum + step_size * step_size * image_norm
    factors[...] = jnp.where(lane == 0, step_size, new_norm / old_norm)

    @pl.when(active)
    def _():
        sent(half1, A1, False)
        sent(half1, A1M, True)
        sent(half2, A2, False)
        sent(half2, A2M, True)
        sent(half3, A3, False)
        sent(half3, A3M, True)
        loop(0, n, lambda b: rc(half3.at[b], half3.at[b], A3S, b, b, sib).wait_send())
        image_copy.wait_send()

        def one(d):
            @pl.when(d != me)
            def _():
                dot_copy(r, d).wait_send()

        loop(0, 2 * n, one)

    @pl.when(idle)
    def _():
        sent(tx, NY, True)


def update(image, factors, iterate, residual, direction, next_iterate, next_residual, next_direction):
    step_size, ratio = factors[:, 0:1], factors[:, 1:2]
    following = residual[...] - step_size * image[...]
    next_residual[...] = following
    next_iterate[...] = iterate[...] + step_size * direction[...]
    next_direction[...] = following + ratio * direction[...]


def local(groups, n, points, centers, inner_factor, outer_factor, iterate, residual, direction):
    pairs, own = n // 2, inner_factor.shape[0]
    count, dims = points.shape
    targets = direction.shape[0]
    half = pltpu.VMEM((pairs, targets, own), bf16)
    block = pltpu.VMEM((targets, own), f32)
    slabs = pltpu.VMEM((n, own, own), bf16)
    whole = pltpu.VMEM((n, targets, own), bf16)
    vmem = pl.BlockSpec(memory_space=pltpu.VMEM)
    anywhere = pl.BlockSpec(memory_space=pl.ANY)
    dma = pltpu.SemaphoreType.DMA
    image, factors = pl.pallas_call(
        functools.partial(kernel, groups, n, count * groups * n),
        out_shape=[jax.ShapeDtypeStruct((targets, own), f32), jax.ShapeDtypeStruct((targets, 128), f32)],
        in_specs=[anywhere] * 4 + [vmem] * 2,
        out_specs=[vmem] * 2,
        scratch_shapes=[
            pltpu.VMEM((n, count, own), bf16), slabs, slabs,
            pltpu.VMEM((count, dims), bf16), pltpu.VMEM((2, own, dims), bf16),
            pltpu.VMEM((count, 2 * dims), bf16), pltpu.VMEM((2 * dims, own), bf16),
            whole, whole, whole,
            pltpu.VMEM((targets, count), f32), pltpu.VMEM((targets, count), bf16), block, block,
            half, pltpu.VMEM((pairs, targets, own), f32), half,
            half, half, half, half, half, half, half,
            pltpu.VMEM((targets, own), bf16), pltpu.VMEM((targets, own), bf16),
            pltpu.VMEM((groups // 2, targets, own) if groups > 2 else (1, 8, 128), f32),
            pltpu.VMEM((n, 8, 128), f32),
            dma((2, n)), dma((3,)), dma((CHANNELS, n)), dma((CHANNELS, n)), dma((2,)),
            dma((max(groups // 2, 1),)), dma((max(groups // 2, 1),)), dma((2 * n,)), dma((n,)),
        ],
        compiler_params=pltpu.CompilerParams(
            collective_id=0, has_side_effects=True, vmem_limit_bytes=63 * 1024 * 1024
        ),
        cost_estimate=pl.CostEstimate(
            flops=2 * count * centers.shape[0] * (dims + 2 * targets),
            bytes_accessed=4 * own * centers.shape[0], transcendentals=count * centers.shape[0]),
    )(points, centers, inner_factor, outer_factor, residual, direction)
    return tuple(pl.pallas_call(
        update,
        out_shape=[jax.ShapeDtypeStruct((targets, own), f32)] * 3,
        in_specs=[vmem] * 5,
        out_specs=[vmem] * 3,
    )(image, factors, iterate, residual, direction))


def solution(mesh):
    placed = (
        P(("grp", "row"), None), P(), P("row", None), P("row", None),
        P(None, "row"), P(None, "row"), P(None, "row"),
    )
    return jax.shard_map(
        functools.partial(local, mesh.shape["grp"], mesh.shape["row"]),
        mesh=mesh,
        in_specs=placed,
        out_specs=(P(None, "row"), P(None, "row"), P(None, "row")),
        check_vma=False,
    )
```

```python
import functools

import jax
import jax.numpy as jnp
from jax import lax
from jax.experimental import pallas as pl
from jax.experimental.pallas import tpu as pltpu
from jax.sharding import PartitionSpec as P

ridge_weight = 0.5
MESH = pl.DeviceIdType.MESH
LAST = (((1,), (1,)), ((), ()))
f32, bf16 = jnp.float32, jnp.bfloat16

(
    A1, A1X, A1S, A2, A2X, A2S, A3, A3X, A3S, A3Y, A3O, A3OX,
    NC, NY, NX, NP, O_S, O_X, O_P, I_S, I_X, I_P, CHANNELS,
) = range(23)
Y1, Y2, YN, YS, YI, SINGLES = range(6)


def nt(a, b):
    return lax.dot_general(a, b, LAST, preferred_element_type=f32)


def mm(a, b):
    return jnp.dot(a, b, preferred_element_type=f32)


def norm_columns(wide, first, other):
    scale = 4.0 / wide.shape[1]
    norms = jnp.minimum(jnp.sum(wide * wide, axis=1, keepdims=True), 3e38) * -scale
    high = norms.astype(bf16).astype(f32)
    mid = (norms - high).astype(bf16).astype(f32)
    low = norms - high - mid
    lane = lax.broadcasted_iota(jnp.int32, wide.shape, 1)
    held = jnp.where(lane == first, high, 0.0)
    held = jnp.where(lane == first + 1, mid, held)
    held = jnp.where(lane == first + 2, low, held)
    held = jnp.where((lane >= other) & (lane < other + 3), 1.0, held)
    return held


def kernel(
    groups, n, point_count,
    points_hbm, centers_hbm, inner_hbm, outer_hbm, residual, direction, image, factors,
    gram, inner_v, outer_v, points_v, centers_v, points_aug, centers_aug,
    half1, half2, own3, oth3, fit, fit_half, acc, ytx1, yrx1, ytx2, yrx2, inner_term,
    ctx, keep, ys, tx, nc_rx, ny_rx, nx_rx, np_rx, os_rx, ox_rx, op_rx, is_rx, ix_rx, ip_rx,
    normal_half, shaped_half, pair_sums, dots,
    lsem, ssem, rsem, ssing, rsing, psend, precv, dsend, drecv,
):
    pairs = n // 2
    own = inner_hbm.shape[0]
    targets = direction.shape[0]
    dims = points_hbm.shape[1]
    g, r = lax.axis_index("grp"), lax.axis_index("row")
    q, c, p = lax.rem(g, 2), lax.rem(r, 2), r // 2
    base = g - q
    active = c == q
    idle = c != q
    sib = (g, r + 1 - 2 * c)
    across = (g + 1 - 2 * q, r)

    rungs, z, x = pairs // 2, p // 2, lax.rem(p, 2)
    beside = 2 * z + 1 - x

    def peer(k):
        return (g, 2 * k + c)

    def column(j):
        return 2 * lax.rem(z + j + 2 * rungs, rungs) + x

    def next_column(j):
        return 2 * lax.rem(z + j + 2 * rungs, rungs) + 1 - x

    def rc(src, dst, ch, si, ri, dev):
        return pltpu.make_async_remote_copy(
            src_ref=src, dst_ref=dst, send_sem=ssem.at[ch, si], recv_sem=rsem.at[ch, ri],
            device_id=dev, device_id_type=MESH)

    def single(src, dst, ch):
        return pltpu.make_async_remote_copy(
            src_ref=src, dst_ref=dst, send_sem=ssing.at[ch], recv_sem=rsing.at[ch],
            device_id=across, device_id_type=MESH)

    def loop(lo, hi, body):
        def step(s, carry):
            body(s)
            return carry
        lax.fori_loop(lo, hi, step, 0)

    points_in = pltpu.make_async_copy(points_hbm, points_v, lsem.at[2, 0])
    centers_in = pltpu.make_async_copy(centers_hbm, centers_v, lsem.at[2, 1])
    points_in.start()
    centers_in.start()

    def slab(factor, held, which, k):
        columns = pl.ds(pl.multiple_of((2 * k + q) * own, own), own)
        return pltpu.make_async_copy(factor.at[:, columns], held.at[k], lsem.at[which, k])

    def load(factor, held, which, s):
        slab(factor, held, which, column(-s)).start()
        slab(factor, held, which, next_column(-s)).start()

    loop(0, rungs, lambda s: load(inner_hbm, inner_v, 0, s))
    loop(0, rungs, lambda s: load(outer_hbm, outer_v, 1, s))

    @pl.when(active)
    def _():
        half1[p] = direction[...].astype(bf16)

    barrier = pltpu.get_barrier_semaphore()

    def greet(d):
        gg, rr = base + d // n, lax.rem(d, n)

        @pl.when((gg != g) | (rr != r))
        def _():
            pl.semaphore_signal(barrier, inc=1, device_id=(gg, rr), device_id_type=MESH)

    loop(0, 2 * n, greet)
    for h in range(groups // 2 if groups > 2 else 0):
        @pl.when(2 * h + q != g)
        def _():
            pl.semaphore_signal(barrier, inc=1, device_id=(2 * h + q, r), device_id_type=MESH)
    pl.semaphore_wait(barrier, 2 * n - 1 + groups // 2 - 1)

    def spread(half, ch):
        @pl.when(active)
        def _():
            rc(half.at[p], half.at[p], ch + 1, p, p, peer(beside)).start()
            loop(1, rungs, lambda j: rc(half.at[p], half.at[p], ch, column(j), p, peer(column(j))).start())
            rc(half.at[p], half.at[p], ch + 2, p, p, sib).start()

    def take_column(half, ch, s):
        k = column(-s)

        @pl.when(active & (s > 0))
        def _():
            rc(half.at[k], half.at[k], ch, k, k, sib).wait_recv()
            rc(half.at[k], half.at[k], ch + 1, k, k, peer(beside)).start()
            rc(half.at[k], half.at[k], ch + 2, k, k, sib).start()

        @pl.when(idle)
        def _():
            rc(half.at[k], half.at[k], ch + 2, k, k, sib).wait_recv()

    def take_next(half, ch, s):
        k = next_column(-s)

        @pl.when(active)
        def _():
            rc(half.at[k], half.at[k], ch + 1, k, k, sib).wait_recv()
            rc(half.at[k], half.at[k], ch + 2, k, k, sib).start()

        @pl.when(idle)
        def _():
            rc(half.at[k], half.at[k], ch + 2, k, k, sib).wait_recv()

    tile = min(512, points_hbm.shape[0])

    def gram_block(b):
        rows = pl.ds(pl.multiple_of(b * own, own), own)
        block = centers_v[rows, :]
        wide = block.astype(f32)
        centers_aug[:dims, :] = wide.T.astype(bf16)
        centers_aug[dims:, :] = norm_columns(wide, 3, 0).T.astype(bf16)
        for i in range(points_hbm.shape[0] // tile):
            at = slice(i * tile, (i + 1) * tile)
            gram[b, at, :] = jnp.exp(mm(points_aug[at, :], centers_aug[...])).astype(bf16)

    spread(half1, A1)
    points_in.wait()
    for i in range(points_hbm.shape[0] // tile):
        at = slice(i * tile, (i + 1) * tile)
        block = points_v[at, :]
        wide = block.astype(f32)
        points_aug[at, :dims] = (wide * (8.0 / dims)).astype(bf16)
        points_aug[at, dims:] = norm_columns(wide, 0, 3).astype(bf16)
    centers_in.wait()

    def product(half, factor, held, which, ch, first):
        acc[...] = jnp.zeros_like(acc)

        def add(k):
            slab(factor, held, which, k).wait()
            acc[...] += nt(half[k], held[k])

        def one(s):
            @pl.when(s < rungs)
            def _():
                take_column(half, ch, s)
                add(column(-s))
                gram_block(first + 2 * s)

            @pl.when(s > 0)
            def _():
                take_next(half, ch, s - 1)
                add(next_column(1 - s))

            @pl.when(s < rungs)
            def _():
                gram_block(first + 2 * s + 1)

        loop(0, rungs + 1, one)

    product(half1, inner_hbm, inner_v, 0, A1, 0)

    @pl.when(idle)
    def _():
        ytx1[...] = acc[...]
        single(ytx1, yrx1, Y1).start()

    @pl.when(active)
    def _():
        single(ytx1, yrx1, Y1).wait_recv()
        total = acc[...] + yrx1[...]
        inner_term[...] = total
        half2[p] = total.astype(bf16)

    spread(half2, A2)
    product(half2, outer_hbm, outer_v, 1, A2, pairs)

    @pl.when(idle)
    def _():
        ytx2[...] = acc[...]
        single(ytx2, yrx2, Y2).start()

    @pl.when(active)
    def _():
        single(ytx2, yrx2, Y2).wait_recv()
        own3[p] = (acc[...] + yrx2[...]).astype(bf16)
        rc(own3.at[p], oth3.at[p], A3Y, p, p, across).start()

    spread(own3, A3)
    fit[...] = jnp.zeros_like(fit)

    def over_x(k):
        return (lax.rem(k, 2) != x) & (lax.rem(k // 2, 2) == 1)

    def to_other(k):
        @pl.when(active & (k != p) & jnp.logical_not(over_x(k)))
        def _():
            rc(own3.at[k], oth3.at[k], A3Y, k, k, across).start()

    def take_other(k):
        @pl.when(idle)
        def _():
            @pl.when(over_x(k))
            def _():
                rc(oth3.at[k], oth3.at[k], A3OX, k, k, sib).wait_recv()

            @pl.when(jnp.logical_not(over_x(k)))
            def _():
                rc(oth3.at[k], oth3.at[k], A3Y, k, k, sib).wait_recv()

            @pl.when((lax.rem(k, 2) == x) & (lax.rem(k // 2, 2) == 1))
            def _():
                rc(oth3.at[k], oth3.at[k], A3OX, k, k, peer(beside)).start()

            rc(oth3.at[k], oth3.at[k], A3O, k, k, sib).start()

        @pl.when(active)
        def _():
            rc(oth3.at[k], oth3.at[k], A3O, k, k, sib).wait_recv()

    def fit_step(s):
        @pl.when(s < rungs)
        def _():
            k = column(-s)
            take_column(own3, A3, s)
            to_other(k)
            fit[...] += nt(own3[k], gram[2 * k + q])

        @pl.when((s >= 1) & (s <= rungs))
        def _():
            k = next_column(1 - s)
            take_next(own3, A3, s - 1)
            to_other(k)
            fit[...] += nt(own3[k], gram[2 * k + q])

        def other(k):
            take_other(k)
            fit[...] += nt(oth3[k], gram[2 * k + 1 - q])

        @pl.when((s >= 1) & (s <= rungs))
        def _():
            other(column(1 - s))

        @pl.when(s >= 2)
        def _():
            other(next_column(2 - s))

    loop(0, rungs + 2, fit_step)
    fit_half[...] = fit[...].astype(bf16)

    def turn(s):
        j = lax.rem(z + 1 + lax.rem(s, rungs), rungs)
        return 2 * j + jnp.where(s < rungs, 1 - x, x)

    def normal_step(s):
        k, k1, k2 = turn(s), turn(jnp.maximum(s - 1, 0)), turn(jnp.maximum(s - 2, 0))

        @pl.when(s < pairs)
        def _():
            ctx[k] = mm(fit_half[...], gram[2 * k + 1 - c]).astype(bf16)
            rc(ctx.at[k], nc_rx.at[k], NC, k, k, sib).start()
            keep[k] = mm(fit_half[...], gram[2 * k + c])

        @pl.when((s >= 1) & (s <= pairs))
        def _():
            rc(ctx.at[k1], nc_rx.at[k1], NC, k1, k1, sib).wait_recv()
            total = keep[k1] + nc_rx[k1].astype(f32)

            @pl.when(idle)
            def _():
                ys[k1] = total.astype(bf16)
                rc(ys.at[k1], ny_rx.at[k1], NY, k1, k1, across).start()

            @pl.when(active)
            def _():
                keep[k1] = total

        @pl.when(active & (s >= 2))
        def _():
            rc(ys.at[k2], ny_rx.at[k2], NY, k2, k2, across).wait_recv()
            deliver(keep[k2] + ny_rx[k2].astype(f32), k2, nx_rx, np_rx, NX)

    def deliver(total, k, x_rx, rx, ch):
        @pl.when(lax.rem(k, 2) != x)
        def _():
            tx[k] = total.astype(bf16)
            rc(tx.at[k], x_rx.at[k], ch, k, k, peer(beside)).start()

        @pl.when(lax.rem(k, 2) == x)
        def _():
            rc(tx.at[k], x_rx.at[k], ch, k, k, peer(beside)).wait_recv()
            both = total + x_rx[k].astype(f32)

            @pl.when(k != p)
            def _():
                tx[k] = both.astype(bf16)
                rc(tx.at[k], rx.at[p], ch + 1, k, p, peer(k)).start()

            @pl.when(k == p)
            def _():
                keep[k] = both

    def collect(rx, ch):
        acc[...] = keep[p]

        def one(j):
            k = column(-j)
            rc(tx.at[k], rx.at[k], ch + 1, k, k, sib).wait_recv()
            acc[...] += rx[k].astype(f32)

        loop(1, rungs, one)

    def delivered(ch):
        loop(0, rungs, lambda j: rc(
            tx.at[next_column(j)], tx.at[next_column(j)], ch, next_column(j), p, sib).wait_send())
        loop(1, rungs, lambda j: rc(
            tx.at[column(j)], tx.at[column(j)], ch + 1, column(j), p, sib).wait_send())

    def sent(src, ch):
        loop(0, pairs, lambda k: rc(src.at[k], src.at[k], ch, k, k, sib).wait_send())

    loop(0, pairs + 2, normal_step)
    sent(ctx, NC)

    @pl.when(active)
    def _():
        collect(np_rx, NX)
        if groups > 2:
            mine = g // 2
            pair_sums[mine] = acc[...]

            def pair_copy(h, to):
                return pltpu.make_async_remote_copy(
                    src_ref=pair_sums.at[h], dst_ref=pair_sums.at[h], send_sem=psend.at[to],
                    recv_sem=precv.at[h], device_id=(2 * to + q, r), device_id_type=MESH)

            for h in range(groups // 2):
                @pl.when(h != mine)
                def _():
                    pair_copy(mine, h).start()
            for h in range(groups // 2):
                @pl.when(h != mine)
                def _():
                    pair_copy(h, h).wait_recv()
            total = pair_sums[0]
            for h in range(1, groups // 2):
                total = total + pair_sums[h]
            acc[...] = total
            for h in range(groups // 2):
                @pl.when(h != mine)
                def _():
                    pair_copy(mine, h).wait_send()
        normal_half[...] = acc[...].astype(bf16)
        single(normal_half, normal_half, YN).start()
        delivered(NX)

    @pl.when(idle)
    def _():
        single(normal_half, normal_half, YN).wait_recv()

    def transposed(held, lhs, s_rx, x_rx, p_rx, ch_s):
        def one(s):
            k, k1 = turn(s), turn(jnp.maximum(s - 1, 0))

            @pl.when(s < pairs)
            def _():
                term = mm(lhs[...], held[k])

                @pl.when(idle)
                def _():
                    ctx[k] = term.astype(bf16)
                    rc(ctx.at[k], s_rx.at[k], ch_s, k, k, sib).start()

                @pl.when(active)
                def _():
                    keep[k] = term

            @pl.when(active & (s >= 1))
            def _():
                rc(ctx.at[k1], s_rx.at[k1], ch_s, k1, k1, sib).wait_recv()
                deliver(keep[k1] + s_rx[k1].astype(f32), k1, x_rx, p_rx, ch_s + 1)

        loop(0, pairs + 1, one)

        @pl.when(active)
        def _():
            collect(p_rx, ch_s + 1)
            delivered(ch_s + 1)

        @pl.when(idle)
        def _():
            sent(ctx, ch_s)

    transposed(outer_v, normal_half, os_rx, ox_rx, op_rx, O_S)

    @pl.when(active)
    def _():
        shaped = acc[...] * (1.0 / point_count) + ridge_weight * inner_term[...]
        shaped_half[...] = shaped.astype(bf16)
        single(shaped_half, shaped_half, YS).start()

    @pl.when(idle)
    def _():
        single(shaped_half, shaped_half, YS).wait_recv()

    transposed(inner_v, shaped_half, is_rx, ix_rx, ip_rx, I_S)

    def dot_copy(slot, d):
        return pltpu.make_async_remote_copy(
            src_ref=dots.at[slot], dst_ref=dots.at[slot], send_sem=dsend.at[d], recv_sem=drecv.at[slot],
            device_id=(base + d // n, lax.rem(d, n)), device_id_type=MESH)

    me = q * n + r
    lane = lax.broadcasted_iota(jnp.int32, (targets, 128), 1)

    @pl.when(active)
    def _():
        image[...] = acc[...]
        x, y, z = acc[...], residual[...], direction[...]
        packed = jnp.zeros((targets, 128), f32)
        for at, pair in enumerate(((y, y), (z, x), (y, x), (x, x))):
            packed = jnp.where(lane == at, jnp.sum(pair[0] * pair[1], axis=1, keepdims=True), packed)
        square = jnp.concatenate([packed, jnp.zeros((128 - targets, 128), f32)], axis=0)
        dots[r] = square.T[:8, :]

        def one(d):
            @pl.when(d != me)
            def _():
                dot_copy(r, d).start()

        loop(0, 2 * n, one)
        single(image, image, YI).start()

    def arrived(slot):
        @pl.when(idle | (slot != r))
        def _():
            dot_copy(slot, me).wait_recv()

    loop(0, n, arrived)
    totals = dots[0]
    for slot in range(1, n):
        totals = totals + dots[slot]
    square = jnp.concatenate([totals, jnp.zeros((120, 128), f32)], axis=0).T

    @pl.when(idle)
    def _():
        single(image, image, YI).wait_recv()

    old_norm, curvature = square[:targets, 0:1], square[:targets, 1:2]
    cross_sum, image_norm = square[:targets, 2:3], square[:targets, 3:4]
    step_size = old_norm / curvature
    new_norm = old_norm - 2.0 * step_size * cross_sum + step_size * step_size * image_norm
    factors[...] = jnp.where(lane == 0, step_size, new_norm / old_norm)

    @pl.when(active)
    def _():
        def gathered(half, ch):
            def forwarded(j, to):
                rc(half.at[column(j)], half.at[p], ch + to, column(j), p, sib).wait_send()

            loop(1, rungs, lambda j: forwarded(j, 0))
            loop(0, rungs, lambda j: forwarded(j, 1))
            sent(half, ch + 2)

        gathered(half1, A1)
        gathered(half2, A2)
        gathered(own3, A3)

        def over_y(k):
            @pl.when(jnp.logical_not(over_x(k)))
            def _():
                rc(own3.at[k], own3.at[k], A3Y, k, k, sib).wait_send()

        loop(0, pairs, over_y)
        single(normal_half, normal_half, YN).wait_send()
        single(shaped_half, shaped_half, YS).wait_send()
        single(image, image, YI).wait_send()

        def one(d):
            @pl.when(d != me)
            def _():
                dot_copy(r, d).wait_send()

        loop(0, 2 * n, one)

    @pl.when(idle)
    def _():
        single(ytx1, yrx1, Y1).wait_send()
        single(ytx2, yrx2, Y2).wait_send()
        sent(oth3, A3O)

        def over_x_sent(j):
            k = column(j)

            @pl.when(lax.rem(k // 2, 2) == 1)
            def _():
                rc(oth3.at[k], oth3.at[k], A3OX, k, k, sib).wait_send()

        loop(0, rungs, over_x_sent)
        sent(ys, NY)


def update(image, factors, iterate, residual, direction, next_iterate, next_residual, next_direction):
    step_size, ratio = factors[:, 0:1], factors[:, 1:2]
    following = residual[...] - step_size * image[...]
    next_residual[...] = following
    next_iterate[...] = iterate[...] + step_size * direction[...]
    next_direction[...] = following + ratio * direction[...]


def local(groups, n, points, centers, inner_factor, outer_factor, iterate, residual, direction):
    pairs, own = n // 2, inner_factor.shape[0]
    count, dims = points.shape
    targets = direction.shape[0]
    half = pltpu.VMEM((pairs, targets, own), bf16)
    block = pltpu.VMEM((targets, own), f32)
    slabs = pltpu.VMEM((pairs, own, own), bf16)
    vmem = pl.BlockSpec(memory_space=pltpu.VMEM)
    anywhere = pl.BlockSpec(memory_space=pl.ANY)
    dma = pltpu.SemaphoreType.DMA
    image, factors = pl.pallas_call(
        functools.partial(kernel, groups, n, count * groups * n),
        out_shape=[jax.ShapeDtypeStruct((targets, own), f32), jax.ShapeDtypeStruct((targets, 128), f32)],
        in_specs=[anywhere] * 4 + [vmem] * 2,
        out_specs=[vmem] * 2,
        scratch_shapes=[
            pltpu.VMEM((n, count, own), bf16), slabs, slabs,
            pltpu.VMEM((count, dims), bf16), pltpu.VMEM(centers.shape, bf16),
            pltpu.VMEM((count, 2 * dims), bf16), pltpu.VMEM((2 * dims, own), bf16),
            half, half, half, half,
            pltpu.VMEM((targets, count), f32), pltpu.VMEM((targets, count), bf16),
            block, block, block, block, block, block,
            half, pltpu.VMEM((pairs, targets, own), f32), half, half,
            half, half, half, half, half, half, half, half, half, half,
            pltpu.VMEM((targets, own), bf16), pltpu.VMEM((targets, own), bf16),
            pltpu.VMEM((max(groups // 2, 1), targets, own) if groups > 2 else (1, 8, 128), f32),
            pltpu.VMEM((n, 8, 128), f32),
            dma((3, max(pairs, 2))), dma((CHANNELS, pairs)), dma((CHANNELS, pairs)),
            dma((SINGLES,)), dma((SINGLES,)),
            dma((max(groups // 2, 1),)), dma((max(groups // 2, 1),)), dma((2 * n,)), dma((n,)),
        ],
        compiler_params=pltpu.CompilerParams(
            collective_id=0, has_side_effects=True, vmem_limit_bytes=60 * 1024 * 1024
        ),
        cost_estimate=pl.CostEstimate(
            flops=2 * count * centers.shape[0] * (dims + 2 * targets),
            bytes_accessed=4 * own * centers.shape[0], transcendentals=count * centers.shape[0]),
    )(points, centers, inner_factor, outer_factor, residual, direction)
    return tuple(pl.pallas_call(
        update,
        out_shape=[jax.ShapeDtypeStruct((targets, own), f32)] * 3,
        in_specs=[vmem] * 5,
        out_specs=[vmem] * 3,
    )(image, factors, iterate, residual, direction))


def solution(mesh):
    placed = (
        P(("grp", "row"), None), P(), P("row", None), P("row", None),
        P(None, "row"), P(None, "row"), P(None, "row"),
    )
    return jax.shard_map(
        functools.partial(local, mesh.shape["grp"], mesh.shape["row"]),
        mesh=mesh,
        in_specs=placed,
        out_specs=(P(None, "row"), P(None, "row"), P(None, "row")),
        check_vma=False,
    )
```

```python
import functools

import jax
import jax.numpy as jnp
from jax import lax
from jax.experimental import pallas as pl
from jax.experimental.pallas import tpu as pltpu
from jax.sharding import PartitionSpec as P

ridge_weight = 0.5
MESH = pl.DeviceIdType.MESH
LAST = (((1,), (1,)), ((), ()))
f32, bf16 = jnp.float32, jnp.bfloat16

A1, A1S, A2, A2S, A3, A3S, A3Y, A3O, NC, NY, NP, O_S, O_P, I_S, I_P, CHANNELS = range(16)
Y1, Y2, YN, YS, YI, SINGLES = range(6)


def nt(a, b):
    return lax.dot_general(a, b, LAST, preferred_element_type=f32)


def mm(a, b):
    return jnp.dot(a, b, preferred_element_type=f32)


def norm_columns(wide, first, other):
    scale = 4.0 / wide.shape[1]
    norms = jnp.minimum(jnp.sum(wide * wide, axis=1, keepdims=True), 3e38) * -scale
    high = norms.astype(bf16).astype(f32)
    mid = (norms - high).astype(bf16).astype(f32)
    low = norms - high - mid
    lane = lax.broadcasted_iota(jnp.int32, wide.shape, 1)
    held = jnp.where(lane == first, high, 0.0)
    held = jnp.where(lane == first + 1, mid, held)
    held = jnp.where(lane == first + 2, low, held)
    held = jnp.where((lane >= other) & (lane < other + 3), 1.0, held)
    return held


def kernel(
    groups, n, point_count,
    points_hbm, centers_hbm, inner_hbm, outer_hbm, residual, direction, image, factors,
    gram, inner_v, outer_v, points_v, centers_v, points_aug, centers_aug,
    half1, half2, own3, oth3, fit, fit_half, acc, ytx1, yrx1, ytx2, yrx2, inner_term,
    ctx, keep, ys, tx, nc_rx, ny_rx, np_rx, os_rx, op_rx, is_rx, ip_rx,
    normal_half, shaped_half, pair_sums, dots,
    lsem, ssem, rsem, ssing, rsing, psend, precv, dsend, drecv,
):
    pairs = n // 2
    own = inner_hbm.shape[0]
    targets = direction.shape[0]
    dims = points_hbm.shape[1]
    g, r = lax.axis_index("grp"), lax.axis_index("row")
    q, c, p = lax.rem(g, 2), lax.rem(r, 2), r // 2
    base = g - q
    active = c == q
    idle = c != q
    sib = (g, r + 1 - 2 * c)
    across = (g + 1 - 2 * q, r)

    def peer(k):
        return (g, 2 * k + q)

    def rc(src, dst, ch, si, ri, dev):
        return pltpu.make_async_remote_copy(
            src_ref=src, dst_ref=dst, send_sem=ssem.at[ch, si], recv_sem=rsem.at[ch, ri],
            device_id=dev, device_id_type=MESH)

    def single(src, dst, ch):
        return pltpu.make_async_remote_copy(
            src_ref=src, dst_ref=dst, send_sem=ssing.at[ch], recv_sem=rsing.at[ch],
            device_id=across, device_id_type=MESH)

    def loop(lo, hi, body):
        def step(s, carry):
            body(s)
            return carry
        lax.fori_loop(lo, hi, step, 0)

    def back(s):
        return lax.rem(p - s + 2 * pairs, pairs)

    def ahead(s):
        return lax.rem(p + 1 + s, pairs)

    points_in = pltpu.make_async_copy(points_hbm, points_v, lsem.at[2, 0])
    centers_in = pltpu.make_async_copy(centers_hbm, centers_v, lsem.at[2, 1])
    points_in.start()
    centers_in.start()

    def slab(factor, held, which, k):
        columns = pl.ds(pl.multiple_of((2 * k + q) * own, own), own)
        return pltpu.make_async_copy(factor.at[:, columns], held.at[k], lsem.at[which, k])

    loop(0, pairs, lambda s: slab(inner_hbm, inner_v, 0, back(s)).start())
    loop(0, pairs, lambda s: slab(outer_hbm, outer_v, 1, back(s)).start())

    @pl.when(active)
    def _():
        half1[p] = direction[...].astype(bf16)

    barrier = pltpu.get_barrier_semaphore()

    def greet(d):
        gg, rr = base + d // n, lax.rem(d, n)

        @pl.when((gg != g) | (rr != r))
        def _():
            pl.semaphore_signal(barrier, inc=1, device_id=(gg, rr), device_id_type=MESH)

    loop(0, 2 * n, greet)
    for h in range(groups // 2 if groups > 2 else 0):
        @pl.when(2 * h + q != g)
        def _():
            pl.semaphore_signal(barrier, inc=1, device_id=(2 * h + q, r), device_id_type=MESH)
    pl.semaphore_wait(barrier, 2 * n - 1 + groups // 2 - 1)

    def spread(half, ch):
        @pl.when(active)
        def _():
            loop(1, pairs, lambda s: rc(
                half.at[p], half.at[p], ch, lax.rem(p + s, pairs), p, peer(lax.rem(p + s, pairs))).start())
            rc(half.at[p], half.at[p], ch + 1, p, p, sib).start()

    def take(half, ch, s, k):
        @pl.when(active & (s > 0))
        def _():
            rc(half.at[k], half.at[k], ch, k, k, sib).wait_recv()
            rc(half.at[k], half.at[k], ch + 1, k, k, sib).start()

        @pl.when(idle)
        def _():
            rc(half.at[k], half.at[k], ch + 1, k, k, sib).wait_recv()

    tile = min(512, points_hbm.shape[0])

    def gram_block(b):
        rows = pl.ds(pl.multiple_of(b * own, own), own)
        block = centers_v[rows, :]
        wide = block.astype(f32)
        centers_aug[:dims, :] = wide.T.astype(bf16)
        centers_aug[dims:, :] = norm_columns(wide, 3, 0).T.astype(bf16)
        for i in range(points_hbm.shape[0] // tile):
            at = slice(i * tile, (i + 1) * tile)
            gram[b, at, :] = jnp.exp(mm(points_aug[at, :], centers_aug[...])).astype(bf16)

    spread(half1, A1)
    points_in.wait()
    for i in range(points_hbm.shape[0] // tile):
        at = slice(i * tile, (i + 1) * tile)
        block = points_v[at, :]
        wide = block.astype(f32)
        points_aug[at, :dims] = (wide * (8.0 / dims)).astype(bf16)
        points_aug[at, dims:] = norm_columns(wide, 0, 3).astype(bf16)
    centers_in.wait()

    acc[...] = jnp.zeros_like(acc)

    def inner_step(s):
        k = back(s)
        take(half1, A1, s, k)
        slab(inner_hbm, inner_v, 0, k).wait()
        acc[...] += nt(half1[k], inner_v[k])
        gram_block(s)

    loop(0, pairs, inner_step)

    @pl.when(idle)
    def _():
        ytx1[...] = acc[...]
        single(ytx1, yrx1, Y1).start()

    @pl.when(active)
    def _():
        single(ytx1, yrx1, Y1).wait_recv()
        total = acc[...] + yrx1[...]
        inner_term[...] = total
        half2[p] = total.astype(bf16)

    spread(half2, A2)
    acc[...] = jnp.zeros_like(acc)

    def outer_step(s):
        k = back(s)
        take(half2, A2, s, k)
        slab(outer_hbm, outer_v, 1, k).wait()
        acc[...] += nt(half2[k], outer_v[k])
        gram_block(pairs + s)

    loop(0, pairs, outer_step)

    @pl.when(idle)
    def _():
        ytx2[...] = acc[...]
        single(ytx2, yrx2, Y2).start()

    @pl.when(active)
    def _():
        single(ytx2, yrx2, Y2).wait_recv()
        own3[p] = (acc[...] + yrx2[...]).astype(bf16)
        rc(own3.at[p], oth3.at[p], A3Y, p, p, across).start()

    spread(own3, A3)
    fit[...] = jnp.zeros_like(fit)

    def fit_add(block, b):
        wide = jnp.concatenate([block.astype(f32), jnp.zeros((128 - targets, own), f32)], axis=0)
        weights = wide.T.astype(bf16)
        for i in range(points_hbm.shape[0] // tile):
            at = slice(i * tile, (i + 1) * tile)
            fit[at, :] += mm(gram[b, at, :], weights)

    def fit_step(s):
        k, k1, k2 = back(s), back(s - 1), back(s - 2)

        @pl.when(s < pairs)
        def _():
            take(own3, A3, s, k)

            @pl.when(active & (s > 0))
            def _():
                rc(own3.at[k], oth3.at[k], A3Y, k, k, across).start()

        @pl.when(idle & (s > 0) & (s <= pairs))
        def _():
            rc(oth3.at[k1], oth3.at[k1], A3Y, k1, k1, across).wait_recv()
            rc(oth3.at[k1], oth3.at[k1], A3O, k1, k1, sib).start()

        @pl.when(s < pairs)
        def _():
            fit_add(own3[k], 2 * k + q)

        @pl.when(s >= 2)
        def _():
            @pl.when(active)
            def _():
                rc(oth3.at[k2], oth3.at[k2], A3O, k2, k2, sib).wait_recv()

            fit_add(oth3[k2], 2 * k2 + 1 - q)

    loop(0, pairs + 2, fit_step)
    fit_half[...] = fit[...].T[:targets, :].astype(bf16)

    def normal_step(s):
        k, k1, k2 = ahead(s), ahead(s - 1 + pairs), ahead(s - 2 + pairs)

        @pl.when(s < pairs)
        def _():
            ctx[k] = mm(fit_half[...], gram[2 * k + 1 - c]).astype(bf16)
            rc(ctx.at[k], nc_rx.at[k], NC, k, k, sib).start()
            keep[k] = mm(fit_half[...], gram[2 * k + c])

        @pl.when((s >= 1) & (s <= pairs))
        def _():
            rc(ctx.at[k1], nc_rx.at[k1], NC, k1, k1, sib).wait_recv()
            total = keep[k1] + nc_rx[k1].astype(f32)

            @pl.when(idle)
            def _():
                ys[k1] = total.astype(bf16)
                rc(ys.at[k1], ny_rx.at[k1], NY, k1, k1, across).start()

            @pl.when(active)
            def _():
                keep[k1] = total

        @pl.when(active & (s >= 2))
        def _():
            rc(ys.at[k2], ny_rx.at[k2], NY, k2, k2, across).wait_recv()
            deliver(keep[k2] + ny_rx[k2].astype(f32), k2, np_rx, NP)

    def deliver(total, k, rx, ch):
        @pl.when(k != p)
        def _():
            tx[k] = total.astype(bf16)
            rc(tx.at[k], rx.at[p], ch, k, p, peer(k)).start()

        @pl.when(k == p)
        def _():
            keep[k] = total

    def collect(rx, ch):
        acc[...] = keep[p]

        def one(s):
            k = back(s)
            rc(tx.at[k], rx.at[k], ch, k, k, sib).wait_recv()
            acc[...] += rx[k].astype(f32)

        loop(1, pairs, one)

    def sent(src, ch, with_own):
        def one(k):
            if with_own:
                rc(src.at[k], src.at[k], ch, k, k, sib).wait_send()
            else:
                @pl.when(k != p)
                def _():
                    rc(src.at[k], src.at[k], ch, k, k, sib).wait_send()
        loop(0, pairs, one)

    loop(0, pairs + 2, normal_step)
    sent(ctx, NC, True)

    @pl.when(active)
    def _():
        collect(np_rx, NP)
        if groups > 2:
            mine = g // 2
            pair_sums[mine] = acc[...]

            def pair_copy(h, to):
                return pltpu.make_async_remote_copy(
                    src_ref=pair_sums.at[h], dst_ref=pair_sums.at[h], send_sem=psend.at[to],
                    recv_sem=precv.at[h], device_id=(2 * to + q, r), device_id_type=MESH)

            for h in range(groups // 2):
                @pl.when(h != mine)
                def _():
                    pair_copy(mine, h).start()
            for h in range(groups // 2):
                @pl.when(h != mine)
                def _():
                    pair_copy(h, h).wait_recv()
            total = pair_sums[0]
            for h in range(1, groups // 2):
                total = total + pair_sums[h]
            acc[...] = total
            for h in range(groups // 2):
                @pl.when(h != mine)
                def _():
                    pair_copy(mine, h).wait_send()
        normal_half[...] = acc[...].astype(bf16)
        single(normal_half, normal_half, YN).start()
        sent(tx, NP, False)

    @pl.when(idle)
    def _():
        single(normal_half, normal_half, YN).wait_recv()

    def transposed(held, lhs, s_rx, p_rx, ch_s, ch_p):
        def one(s):
            k, k1 = ahead(s), ahead(s - 1 + pairs)

            @pl.when(s < pairs)
            def _():
                term = mm(lhs[...], held[k])

                @pl.when(idle)
                def _():
                    ctx[k] = term.astype(bf16)
                    rc(ctx.at[k], s_rx.at[k], ch_s, k, k, sib).start()

                @pl.when(active)
                def _():
                    keep[k] = term

            @pl.when(active & (s >= 1))
            def _():
                rc(ctx.at[k1], s_rx.at[k1], ch_s, k1, k1, sib).wait_recv()
                deliver(keep[k1] + s_rx[k1].astype(f32), k1, p_rx, ch_p)

        loop(0, pairs + 1, one)

        @pl.when(active)
        def _():
            collect(p_rx, ch_p)
            sent(tx, ch_p, False)

        @pl.when(idle)
        def _():
            sent(ctx, ch_s, True)

    transposed(outer_v, normal_half, os_rx, op_rx, O_S, O_P)

    @pl.when(active)
    def _():
        shaped = acc[...] * (1.0 / point_count) + ridge_weight * inner_term[...]
        shaped_half[...] = shaped.astype(bf16)
        single(shaped_half, shaped_half, YS).start()

    @pl.when(idle)
    def _():
        single(shaped_half, shaped_half, YS).wait_recv()

    transposed(inner_v, shaped_half, is_rx, ip_rx, I_S, I_P)

    def dot_copy(slot, d):
        return pltpu.make_async_remote_copy(
            src_ref=dots.at[slot], dst_ref=dots.at[slot], send_sem=dsend.at[d], recv_sem=drecv.at[slot],
            device_id=(base + d // n, lax.rem(d, n)), device_id_type=MESH)

    me = q * n + r
    lane = lax.broadcasted_iota(jnp.int32, (targets, 128), 1)

    @pl.when(active)
    def _():
        image[...] = acc[...]
        x, y, z = acc[...], residual[...], direction[...]
        packed = jnp.zeros((targets, 128), f32)
        for at, pair in enumerate(((y, y), (z, x), (y, x), (x, x))):
            packed = jnp.where(lane == at, jnp.sum(pair[0] * pair[1], axis=1, keepdims=True), packed)
        square = jnp.concatenate([packed, jnp.zeros((128 - targets, 128), f32)], axis=0)
        dots[r] = square.T[:8, :]

        def one(d):
            @pl.when(d != me)
            def _():
                dot_copy(r, d).start()

        loop(0, 2 * n, one)
        single(image, image, YI).start()

    def arrived(slot):
        @pl.when(idle | (slot != r))
        def _():
            dot_copy(slot, me).wait_recv()

    loop(0, n, arrived)
    totals = dots[0]
    for slot in range(1, n):
        totals = totals + dots[slot]
    square = jnp.concatenate([totals, jnp.zeros((120, 128), f32)], axis=0).T

    @pl.when(idle)
    def _():
        single(image, image, YI).wait_recv()

    old_norm, curvature = square[:targets, 0:1], square[:targets, 1:2]
    cross_sum, image_norm = square[:targets, 2:3], square[:targets, 3:4]
    step_size = old_norm / curvature
    new_norm = old_norm - 2.0 * step_size * cross_sum + step_size * step_size * image_norm
    factors[...] = jnp.where(lane == 0, step_size, new_norm / old_norm)

    @pl.when(active)
    def _():
        sent(half1, A1, False)
        sent(half1, A1S, True)
        sent(half2, A2, False)
        sent(half2, A2S, True)
        sent(own3, A3, False)
        sent(own3, A3S, True)
        sent(own3, A3Y, True)
        single(normal_half, normal_half, YN).wait_send()
        single(shaped_half, shaped_half, YS).wait_send()
        single(image, image, YI).wait_send()

        def one(d):
            @pl.when(d != me)
            def _():
                dot_copy(r, d).wait_send()

        loop(0, 2 * n, one)

    @pl.when(idle)
    def _():
        single(ytx1, yrx1, Y1).wait_send()
        single(ytx2, yrx2, Y2).wait_send()
        sent(oth3, A3O, True)
        sent(ys, NY, True)


def update(image, factors, iterate, residual, direction, next_iterate, next_residual, next_direction):
    step_size, ratio = factors[:, 0:1], factors[:, 1:2]
    following = residual[...] - step_size * image[...]
    next_residual[...] = following
    next_iterate[...] = iterate[...] + step_size * direction[...]
    next_direction[...] = following + ratio * direction[...]


def local(groups, n, points, centers, inner_factor, outer_factor, iterate, residual, direction):
    pairs, own = n // 2, inner_factor.shape[0]
    count, dims = points.shape
    targets = direction.shape[0]
    half = pltpu.VMEM((pairs, targets, own), bf16)
    block = pltpu.VMEM((targets, own), f32)
    slabs = pltpu.VMEM((pairs, own, own), bf16)
    vmem = pl.BlockSpec(memory_space=pltpu.VMEM)
    anywhere = pl.BlockSpec(memory_space=pl.ANY)
    dma = pltpu.SemaphoreType.DMA
    image, factors = pl.pallas_call(
        functools.partial(kernel, groups, n, count * groups * n),
        out_shape=[jax.ShapeDtypeStruct((targets, own), f32), jax.ShapeDtypeStruct((targets, 128), f32)],
        in_specs=[anywhere] * 4 + [vmem] * 2,
        out_specs=[vmem] * 2,
        scratch_shapes=[
            pltpu.VMEM((n, count, own), bf16), slabs, slabs,
            pltpu.VMEM((count, dims), bf16), pltpu.VMEM(centers.shape, bf16),
            pltpu.VMEM((count, 2 * dims), bf16), pltpu.VMEM((2 * dims, own), bf16),
            half, half, half, half,
            pltpu.VMEM((count, 128), f32), pltpu.VMEM((targets, count), bf16),
            block, block, block, block, block, block,
            half, pltpu.VMEM((pairs, targets, own), f32), half, half,
            half, half, half, half, half, half, half,
            pltpu.VMEM((targets, own), bf16), pltpu.VMEM((targets, own), bf16),
            pltpu.VMEM((max(groups // 2, 1), targets, own) if groups > 2 else (1, 8, 128), f32),
            pltpu.VMEM((n, 8, 128), f32),
            dma((3, max(pairs, 2))), dma((CHANNELS, pairs)), dma((CHANNELS, pairs)),
            dma((SINGLES,)), dma((SINGLES,)),
            dma((max(groups // 2, 1),)), dma((max(groups // 2, 1),)), dma((2 * n,)), dma((n,)),
        ],
        compiler_params=pltpu.CompilerParams(
            collective_id=0, has_side_effects=True, vmem_limit_bytes=60 * 1024 * 1024
        ),
        cost_estimate=pl.CostEstimate(
            flops=2 * count * centers.shape[0] * (dims + 2 * targets),
            bytes_accessed=4 * own * centers.shape[0], transcendentals=count * centers.shape[0]),
    )(points, centers, inner_factor, outer_factor, residual, direction)
    return tuple(pl.pallas_call(
        update,
        out_shape=[jax.ShapeDtypeStruct((targets, own), f32)] * 3,
        in_specs=[vmem] * 5,
        out_specs=[vmem] * 3,
    )(image, factors, iterate, residual, direction))


def solution(mesh):
    placed = (
        P(("grp", "row"), None), P(), P("row", None), P("row", None),
        P(None, "row"), P(None, "row"), P(None, "row"),
    )
    return jax.shard_map(
        functools.partial(local, mesh.shape["grp"], mesh.shape["row"]),
        mesh=mesh,
        in_specs=placed,
        out_specs=(P(None, "row"), P(None, "row"), P(None, "row")),
        check_vma=False,
    )
```

```python
import functools

import jax
import jax.numpy as jnp
from jax import lax
from jax.experimental import pallas as pl
from jax.experimental.pallas import tpu as pltpu
from jax.sharding import PartitionSpec as P

ridge_weight = 0.5
MESH = pl.DeviceIdType.MESH
LAST = (((1,), (1,)), ((), ()))
f32, bf16 = jnp.float32, jnp.bfloat16

A1, A1S, A2, A2S, A3, A3S, A3Y, A3O, NC, NY, NP, O_S, O_P, I_S, I_P, CHANNELS = range(16)
Y1, Y2, YN, YS, YI, SINGLES = range(6)


def nt(a, b):
    return lax.dot_general(a, b, LAST, preferred_element_type=f32)


def mm(a, b):
    return jnp.dot(a, b, preferred_element_type=f32)


def norm_columns(wide, first, other):
    scale = 4.0 / wide.shape[1]
    norms = jnp.minimum(jnp.sum(wide * wide, axis=1, keepdims=True), 3e38) * -scale
    high = norms.astype(bf16).astype(f32)
    mid = (norms - high).astype(bf16).astype(f32)
    low = norms - high - mid
    lane = lax.broadcasted_iota(jnp.int32, wide.shape, 1)
    held = jnp.where(lane == first, high, 0.0)
    held = jnp.where(lane == first + 1, mid, held)
    held = jnp.where(lane == first + 2, low, held)
    held = jnp.where((lane >= other) & (lane < other + 3), 1.0, held)
    return held


def kernel(
    groups, n, point_count,
    points_hbm, centers_hbm, inner_hbm, outer_hbm, residual, direction, image, factors,
    gram, inner_v, outer_v, points_v, centers_v, points_aug, centers_aug,
    half1, half2, own3, oth3, fit, fit_half, acc, ytx1, yrx1, ytx2, yrx2, inner_term,
    ctx, keep, ys, tx, nc_rx, ny_rx, np_rx, os_rx, op_rx, is_rx, ip_rx,
    normal_half, shaped_half, pair_sums, dots,
    lsem, ssem, rsem, ssing, rsing, psend, precv, dsend, drecv,
):
    pairs = n // 2
    own = inner_hbm.shape[0]
    targets = direction.shape[0]
    dims = points_hbm.shape[1]
    g, r = lax.axis_index("grp"), lax.axis_index("row")
    q, c, p = lax.rem(g, 2), lax.rem(r, 2), r // 2
    base = g - q
    active = c == q
    idle = c != q
    sib = (g, r + 1 - 2 * c)
    across = (g + 1 - 2 * q, r)

    def peer(k):
        return (g, 2 * k + q)

    def rc(src, dst, ch, si, ri, dev):
        return pltpu.make_async_remote_copy(
            src_ref=src, dst_ref=dst, send_sem=ssem.at[ch, si], recv_sem=rsem.at[ch, ri],
            device_id=dev, device_id_type=MESH)

    def single(src, dst, ch):
        return pltpu.make_async_remote_copy(
            src_ref=src, dst_ref=dst, send_sem=ssing.at[ch], recv_sem=rsing.at[ch],
            device_id=across, device_id_type=MESH)

    def loop(lo, hi, body):
        def step(s, carry):
            body(s)
            return carry
        lax.fori_loop(lo, hi, step, 0)

    def back(s):
        return lax.rem(p - s + 2 * pairs, pairs)

    def ahead(s):
        return lax.rem(p + 1 + s, pairs)

    points_in = pltpu.make_async_copy(points_hbm, points_v, lsem.at[2, 0])
    centers_in = pltpu.make_async_copy(centers_hbm, centers_v, lsem.at[2, 1])
    points_in.start()
    centers_in.start()

    def slab(factor, held, which, k):
        columns = pl.ds(pl.multiple_of((2 * k + q) * own, own), own)
        return pltpu.make_async_copy(factor.at[:, columns], held.at[k], lsem.at[which, k])

    loop(0, pairs, lambda s: slab(inner_hbm, inner_v, 0, back(s)).start())
    loop(0, pairs, lambda s: slab(outer_hbm, outer_v, 1, back(s)).start())

    @pl.when(active)
    def _():
        half1[p] = direction[...].astype(bf16)

    barrier = pltpu.get_barrier_semaphore()

    def greet(d):
        gg, rr = base + d // n, lax.rem(d, n)

        @pl.when((gg != g) | (rr != r))
        def _():
            pl.semaphore_signal(barrier, inc=1, device_id=(gg, rr), device_id_type=MESH)

    loop(0, 2 * n, greet)
    for h in range(groups // 2 if groups > 2 else 0):
        @pl.when(2 * h + q != g)
        def _():
            pl.semaphore_signal(barrier, inc=1, device_id=(2 * h + q, r), device_id_type=MESH)

    def spread(half, ch):
        @pl.when(active)
        def _():
            loop(1, pairs, lambda s: rc(
                half.at[p], half.at[p], ch, lax.rem(p + s, pairs), p, peer(lax.rem(p + s, pairs))).start())
            rc(half.at[p], half.at[p], ch + 1, p, p, sib).start()

    def take(half, ch, s, k):
        @pl.when(active & (s > 0))
        def _():
            rc(half.at[k], half.at[k], ch, k, k, sib).wait_recv()
            rc(half.at[k], half.at[k], ch + 1, k, k, sib).start()

        @pl.when(idle)
        def _():
            rc(half.at[k], half.at[k], ch + 1, k, k, sib).wait_recv()

    tile = min(512, points_hbm.shape[0])

    def gram_block(b):
        rows = pl.ds(pl.multiple_of(b * own, own), own)
        block = centers_v[rows, :]
        wide = block.astype(f32)
        centers_aug[:dims, :] = wide.T.astype(bf16)
        centers_aug[dims:, :] = norm_columns(wide, 3, 0).T.astype(bf16)
        for i in range(points_hbm.shape[0] // tile):
            at = slice(i * tile, (i + 1) * tile)
            gram[b, at, :] = jnp.exp(mm(points_aug[at, :], centers_aug[...])).astype(bf16)

    points_in.wait()
    for i in range(points_hbm.shape[0] // tile):
        at = slice(i * tile, (i + 1) * tile)
        block = points_v[at, :]
        wide = block.astype(f32)
        points_aug[at, :dims] = (wide * (8.0 / dims)).astype(bf16)
        points_aug[at, dims:] = norm_columns(wide, 0, 3).astype(bf16)
    centers_in.wait()

    unit = n // 16
    marks = [0, unit, 6 * unit, 8 * unit, 13 * unit, 15 * unit, n]

    def gram_blocks(place):
        loop(marks[place], marks[place + 1], gram_block)

    gram_blocks(0)
    pl.semaphore_wait(barrier, 2 * n - 1 + groups // 2 - 1)
    spread(half1, A1)

    acc[...] = jnp.zeros_like(acc)

    def inner_step(s):
        k = back(s)
        take(half1, A1, s, k)
        slab(inner_hbm, inner_v, 0, k).wait()
        acc[...] += nt(half1[k], inner_v[k])

        @pl.when(s < marks[2] - marks[1])
        def _():
            gram_block(marks[1] + s)

    loop(0, pairs, inner_step)

    @pl.when(idle)
    def _():
        ytx1[...] = acc[...]
        single(ytx1, yrx1, Y1).start()

    gram_blocks(2)

    @pl.when(active)
    def _():
        single(ytx1, yrx1, Y1).wait_recv()
        total = acc[...] + yrx1[...]
        inner_term[...] = total
        half2[p] = total.astype(bf16)

    spread(half2, A2)
    acc[...] = jnp.zeros_like(acc)

    def outer_step(s):
        k = back(s)
        take(half2, A2, s, k)
        slab(outer_hbm, outer_v, 1, k).wait()
        acc[...] += nt(half2[k], outer_v[k])

        @pl.when(s < marks[4] - marks[3])
        def _():
            gram_block(marks[3] + s)

    loop(0, pairs, outer_step)

    @pl.when(idle)
    def _():
        ytx2[...] = acc[...]
        single(ytx2, yrx2, Y2).start()

    gram_blocks(4)

    @pl.when(active)
    def _():
        single(ytx2, yrx2, Y2).wait_recv()
        own3[p] = (acc[...] + yrx2[...]).astype(bf16)
        rc(own3.at[p], oth3.at[p], A3Y, p, p, across).start()

    spread(own3, A3)
    gram_blocks(5)
    fit[...] = jnp.zeros_like(fit)

    def fit_step(s):
        k, k1, k2 = back(s), back(s - 1), back(s - 2)

        @pl.when(s < pairs)
        def _():
            take(own3, A3, s, k)

            @pl.when(active & (s > 0))
            def _():
                rc(own3.at[k], oth3.at[k], A3Y, k, k, across).start()

        @pl.when(idle & (s > 0) & (s <= pairs))
        def _():
            rc(oth3.at[k1], oth3.at[k1], A3Y, k1, k1, across).wait_recv()
            rc(oth3.at[k1], oth3.at[k1], A3O, k1, k1, sib).start()

        @pl.when(s < pairs)
        def _():
            fit[...] += nt(own3[k], gram[2 * k + q])

        @pl.when(s >= 2)
        def _():
            @pl.when(active)
            def _():
                rc(oth3.at[k2], oth3.at[k2], A3O, k2, k2, sib).wait_recv()

            fit[...] += nt(oth3[k2], gram[2 * k2 + 1 - q])

    loop(0, pairs + 2, fit_step)
    fit_half[...] = fit[...].astype(bf16)

    def normal_step(s):
        k, k1, k2 = ahead(s), ahead(s - 1 + pairs), ahead(s - 2 + pairs)

        @pl.when(s < pairs)
        def _():
            ctx[k] = mm(fit_half[...], gram[2 * k + 1 - c]).astype(bf16)
            rc(ctx.at[k], nc_rx.at[k], NC, k, k, sib).start()
            keep[k] = mm(fit_half[...], gram[2 * k + c])

        @pl.when((s >= 1) & (s <= pairs))
        def _():
            rc(ctx.at[k1], nc_rx.at[k1], NC, k1, k1, sib).wait_recv()
            total = keep[k1] + nc_rx[k1].astype(f32)

            @pl.when(idle)
            def _():
                ys[k1] = total.astype(bf16)
                rc(ys.at[k1], ny_rx.at[k1], NY, k1, k1, across).start()

            @pl.when(active)
            def _():
                keep[k1] = total

        @pl.when(active & (s >= 2))
        def _():
            rc(ys.at[k2], ny_rx.at[k2], NY, k2, k2, across).wait_recv()
            deliver(keep[k2] + ny_rx[k2].astype(f32), k2, np_rx, NP)

    def deliver(total, k, rx, ch):
        @pl.when(k != p)
        def _():
            tx[k] = total.astype(bf16)
            rc(tx.at[k], rx.at[p], ch, k, p, peer(k)).start()

        @pl.when(k == p)
        def _():
            keep[k] = total

    def collect(rx, ch):
        acc[...] = keep[p]

        def one(s):
            k = back(s)
            rc(tx.at[k], rx.at[k], ch, k, k, sib).wait_recv()
            acc[...] += rx[k].astype(f32)

        loop(1, pairs, one)

    def sent(src, ch, with_own):
        def one(k):
            if with_own:
                rc(src.at[k], src.at[k], ch, k, k, sib).wait_send()
            else:
                @pl.when(k != p)
                def _():
                    rc(src.at[k], src.at[k], ch, k, k, sib).wait_send()
        loop(0, pairs, one)

    loop(0, pairs + 2, normal_step)
    sent(ctx, NC, True)

    @pl.when(active)
    def _():
        collect(np_rx, NP)
        if groups > 2:
            mine = g // 2
            pair_sums[mine] = acc[...]

            def pair_copy(h, to):
                return pltpu.make_async_remote_copy(
                    src_ref=pair_sums.at[h], dst_ref=pair_sums.at[h], send_sem=psend.at[to],
                    recv_sem=precv.at[h], device_id=(2 * to + q, r), device_id_type=MESH)

            for h in range(groups // 2):
                @pl.when(h != mine)
                def _():
                    pair_copy(mine, h).start()
            for h in range(groups // 2):
                @pl.when(h != mine)
                def _():
                    pair_copy(h, h).wait_recv()
            total = pair_sums[0]
            for h in range(1, groups // 2):
                total = total + pair_sums[h]
            acc[...] = total
            for h in range(groups // 2):
                @pl.when(h != mine)
                def _():
                    pair_copy(mine, h).wait_send()
        normal_half[...] = acc[...].astype(bf16)
        single(normal_half, normal_half, YN).start()
        sent(tx, NP, False)

    @pl.when(idle)
    def _():
        single(normal_half, normal_half, YN).wait_recv()

    def transposed(held, lhs, s_rx, p_rx, ch_s, ch_p):
        def one(s):
            k, k1 = ahead(s), ahead(s - 1 + pairs)

            @pl.when(s < pairs)
            def _():
                term = mm(lhs[...], held[k])

                @pl.when(idle)
                def _():
                    ctx[k] = term.astype(bf16)
                    rc(ctx.at[k], s_rx.at[k], ch_s, k, k, sib).start()

                @pl.when(active)
                def _():
                    keep[k] = term

            @pl.when(active & (s >= 1))
            def _():
                rc(ctx.at[k1], s_rx.at[k1], ch_s, k1, k1, sib).wait_recv()
                deliver(keep[k1] + s_rx[k1].astype(f32), k1, p_rx, ch_p)

        loop(0, pairs + 1, one)

        @pl.when(active)
        def _():
            collect(p_rx, ch_p)
            sent(tx, ch_p, False)

        @pl.when(idle)
        def _():
            sent(ctx, ch_s, True)

    transposed(outer_v, normal_half, os_rx, op_rx, O_S, O_P)

    @pl.when(active)
    def _():
        shaped = acc[...] * (1.0 / point_count) + ridge_weight * inner_term[...]
        shaped_half[...] = shaped.astype(bf16)
        single(shaped_half, shaped_half, YS).start()

    @pl.when(idle)
    def _():
        single(shaped_half, shaped_half, YS).wait_recv()

    transposed(inner_v, shaped_half, is_rx, ip_rx, I_S, I_P)

    def dot_copy(slot, d):
        return pltpu.make_async_remote_copy(
            src_ref=dots.at[slot], dst_ref=dots.at[slot], send_sem=dsend.at[d], recv_sem=drecv.at[slot],
            device_id=(base + d // n, lax.rem(d, n)), device_id_type=MESH)

    me = q * n + r
    lane = lax.broadcasted_iota(jnp.int32, (targets, 128), 1)

    @pl.when(active)
    def _():
        image[...] = acc[...]
        x, y, z = acc[...], residual[...], direction[...]
        packed = jnp.zeros((targets, 128), f32)
        for at, pair in enumerate(((y, y), (z, x), (y, x), (x, x))):
            packed = jnp.where(lane == at, jnp.sum(pair[0] * pair[1], axis=1, keepdims=True), packed)
        square = jnp.concatenate([packed, jnp.zeros((128 - targets, 128), f32)], axis=0)
        dots[r] = square.T[:8, :]

        def one(d):
            @pl.when(d != me)
            def _():
                dot_copy(r, d).start()

        loop(0, 2 * n, one)
        single(image, image, YI).start()

    def arrived(slot):
        @pl.when(idle | (slot != r))
        def _():
            dot_copy(slot, me).wait_recv()

    loop(0, n, arrived)
    totals = dots[0]
    for slot in range(1, n):
        totals = totals + dots[slot]
    square = jnp.concatenate([totals, jnp.zeros((120, 128), f32)], axis=0).T

    @pl.when(idle)
    def _():
        single(image, image, YI).wait_recv()

    old_norm, curvature = square[:targets, 0:1], square[:targets, 1:2]
    cross_sum, image_norm = square[:targets, 2:3], square[:targets, 3:4]
    step_size = old_norm / curvature
    new_norm = old_norm - 2.0 * step_size * cross_sum + step_size * step_size * image_norm
    factors[...] = jnp.where(lane == 0, step_size, new_norm / old_norm)

    @pl.when(active)
    def _():
        sent(half1, A1, False)
        sent(half1, A1S, True)
        sent(half2, A2, False)
        sent(half2, A2S, True)
        sent(own3, A3, False)
        sent(own3, A3S, True)
        sent(own3, A3Y, True)
        single(normal_half, normal_half, YN).wait_send()
        single(shaped_half, shaped_half, YS).wait_send()
        single(image, image, YI).wait_send()

        def one(d):
            @pl.when(d != me)
            def _():
                dot_copy(r, d).wait_send()

        loop(0, 2 * n, one)

    @pl.when(idle)
    def _():
        single(ytx1, yrx1, Y1).wait_send()
        single(ytx2, yrx2, Y2).wait_send()
        sent(oth3, A3O, True)
        sent(ys, NY, True)


def update(image, factors, iterate, residual, direction, next_iterate, next_residual, next_direction):
    step_size, ratio = factors[:, 0:1], factors[:, 1:2]
    following = residual[...] - step_size * image[...]
    next_residual[...] = following
    next_iterate[...] = iterate[...] + step_size * direction[...]
    next_direction[...] = following + ratio * direction[...]


def local(groups, n, points, centers, inner_factor, outer_factor, iterate, residual, direction):
    pairs, own = n // 2, inner_factor.shape[0]
    count, dims = points.shape
    targets = direction.shape[0]
    half = pltpu.VMEM((pairs, targets, own), bf16)
    block = pltpu.VMEM((targets, own), f32)
    slabs = pltpu.VMEM((pairs, own, own), bf16)
    vmem = pl.BlockSpec(memory_space=pltpu.VMEM)
    anywhere = pl.BlockSpec(memory_space=pl.ANY)
    dma = pltpu.SemaphoreType.DMA
    image, factors = pl.pallas_call(
        functools.partial(kernel, groups, n, count * groups * n),
        out_shape=[jax.ShapeDtypeStruct((targets, own), f32), jax.ShapeDtypeStruct((targets, 128), f32)],
        in_specs=[anywhere] * 4 + [vmem] * 2,
        out_specs=[vmem] * 2,
        scratch_shapes=[
            pltpu.VMEM((n, count, own), bf16), slabs, slabs,
            pltpu.VMEM((count, dims), bf16), pltpu.VMEM(centers.shape, bf16),
            pltpu.VMEM((count, 2 * dims), bf16), pltpu.VMEM((2 * dims, own), bf16),
            half, half, half, half,
            pltpu.VMEM((targets, count), f32), pltpu.VMEM((targets, count), bf16),
            block, block, block, block, block, block,
            half, pltpu.VMEM((pairs, targets, own), f32), half, half,
            half, half, half, half, half, half, half,
            pltpu.VMEM((targets, own), bf16), pltpu.VMEM((targets, own), bf16),
            pltpu.VMEM((max(groups // 2, 1), targets, own) if groups > 2 else (1, 8, 128), f32),
            pltpu.VMEM((n, 8, 128), f32),
            dma((3, max(pairs, 2))), dma((CHANNELS, pairs)), dma((CHANNELS, pairs)),
            dma((SINGLES,)), dma((SINGLES,)),
            dma((max(groups // 2, 1),)), dma((max(groups // 2, 1),)), dma((2 * n,)), dma((n,)),
        ],
        compiler_params=pltpu.CompilerParams(
            collective_id=0, has_side_effects=True, vmem_limit_bytes=60 * 1024 * 1024
        ),
        cost_estimate=pl.CostEstimate(
            flops=2 * count * centers.shape[0] * (dims + 2 * targets),
            bytes_accessed=4 * own * centers.shape[0], transcendentals=count * centers.shape[0]),
    )(points, centers, inner_factor, outer_factor, residual, direction)
    return tuple(pl.pallas_call(
        update,
        out_shape=[jax.ShapeDtypeStruct((targets, own), f32)] * 3,
        in_specs=[vmem] * 5,
        out_specs=[vmem] * 3,
    )(image, factors, iterate, residual, direction))


def solution(mesh):
    placed = (
        P(("grp", "row"), None), P(), P("row", None), P("row", None),
        P(None, "row"), P(None, "row"), P(None, "row"),
    )
    return jax.shard_map(
        functools.partial(local, mesh.shape["grp"], mesh.shape["row"]),
        mesh=mesh,
        in_specs=placed,
        out_specs=(P(None, "row"), P(None, "row"), P(None, "row")),
        check_vma=False,
    )
```

```python
import functools
import math

import jax
import jax.numpy as jnp
from jax import lax
from jax.experimental import pallas as pl
from jax.experimental.pallas import tpu as pltpu
from jax.sharding import PartitionSpec as P

ridge_weight = 0.5
MESH = pl.DeviceIdType.MESH
LAST = (((1,), (1,)), ((), ()))
f32, bf16 = jnp.float32, jnp.bfloat16

A1, A1S, A2, A2S, A3, A3S, A3Y, A3O, NC, NY, NP, O_S, O_P, I_S, I_P, CHANNELS = range(16)
Y1, Y2, YN, YS, YI, SINGLES = range(6)


def nt(a, b):
    return lax.dot_general(a, b, LAST, preferred_element_type=f32)


def mm(a, b):
    return jnp.dot(a, b, preferred_element_type=f32)


def norm_columns(wide, first, other):
    scale = 4.0 / wide.shape[1]
    norms = jnp.minimum(jnp.sum(wide * wide, axis=1, keepdims=True), 3e38) * -scale
    high = norms.astype(bf16).astype(f32)
    mid = (norms - high).astype(bf16).astype(f32)
    low = norms - high - mid
    lane = lax.broadcasted_iota(jnp.int32, wide.shape, 1)
    held = jnp.where(lane == first, high, 0.0)
    held = jnp.where(lane == first + 1, mid, held)
    held = jnp.where(lane == first + 2, low, held)
    held = jnp.where((lane >= other) & (lane < other + 3), 1.0, held)
    return held


def exponential(power):
    y = jnp.maximum(power * math.log2(math.e), -160.0)
    coarse = y.astype(bf16)
    left = (y - coarse.astype(f32)).astype(bf16)
    scale = jnp.exp2(coarse)
    ln2 = math.log(2.0)
    series = left * (left * bf16(0.5 * ln2 * ln2) + bf16(ln2))
    return scale + scale * series


def kernel(
    groups, n, point_count,
    points_hbm, centers_hbm, inner_hbm, outer_hbm, residual, direction, image, factors,
    gram, inner_v, outer_v, points_v, centers_v, points_aug, centers_aug,
    half1, half2, own3, oth3, fit, fit_half, acc, ytx1, yrx1, ytx2, yrx2, inner_term,
    ctx, keep, ys, tx, nc_rx, ny_rx, np_rx, os_rx, op_rx, is_rx, ip_rx,
    normal_half, shaped_half, pair_sums, dots,
    lsem, ssem, rsem, ssing, rsing, psend, precv, dsend, drecv,
):
    pairs = n // 2
    own = inner_hbm.shape[0]
    targets = direction.shape[0]
    dims = points_hbm.shape[1]
    g, r = lax.axis_index("grp"), lax.axis_index("row")
    q, c, p = lax.rem(g, 2), lax.rem(r, 2), r // 2
    base = g - q
    active = c == q
    idle = c != q
    sib = (g, r + 1 - 2 * c)
    across = (g + 1 - 2 * q, r)

    def peer(k):
        return (g, 2 * k + q)

    def rc(src, dst, ch, si, ri, dev):
        return pltpu.make_async_remote_copy(
            src_ref=src, dst_ref=dst, send_sem=ssem.at[ch, si], recv_sem=rsem.at[ch, ri],
            device_id=dev, device_id_type=MESH)

    def single(src, dst, ch):
        return pltpu.make_async_remote_copy(
            src_ref=src, dst_ref=dst, send_sem=ssing.at[ch], recv_sem=rsing.at[ch],
            device_id=across, device_id_type=MESH)

    def loop(lo, hi, body):
        def step(s, carry):
            body(s)
            return carry
        lax.fori_loop(lo, hi, step, 0)

    def back(s):
        return lax.rem(p - s + 2 * pairs, pairs)

    def ahead(s):
        return lax.rem(p + 1 + s, pairs)

    points_in = pltpu.make_async_copy(points_hbm, points_v, lsem.at[2, 0])
    centers_in = pltpu.make_async_copy(centers_hbm, centers_v, lsem.at[2, 1])
    points_in.start()
    centers_in.start()

    def slab(factor, held, which, k):
        columns = pl.ds(pl.multiple_of((2 * k + q) * own, own), own)
        return pltpu.make_async_copy(factor.at[:, columns], held.at[k], lsem.at[which, k])

    loop(0, pairs, lambda s: slab(inner_hbm, inner_v, 0, back(s)).start())
    loop(0, pairs, lambda s: slab(outer_hbm, outer_v, 1, back(s)).start())

    @pl.when(active)
    def _():
        half1[p] = direction[...].astype(bf16)

    barrier = pltpu.get_barrier_semaphore()

    def greet(d):
        gg, rr = base + d // n, lax.rem(d, n)

        @pl.when((gg != g) | (rr != r))
        def _():
            pl.semaphore_signal(barrier, inc=1, device_id=(gg, rr), device_id_type=MESH)

    loop(0, 2 * n, greet)
    for h in range(groups // 2 if groups > 2 else 0):
        @pl.when(2 * h + q != g)
        def _():
            pl.semaphore_signal(barrier, inc=1, device_id=(2 * h + q, r), device_id_type=MESH)

    def spread(half, ch):
        @pl.when(active)
        def _():
            loop(1, pairs, lambda s: rc(
                half.at[p], half.at[p], ch, lax.rem(p + s, pairs), p, peer(lax.rem(p + s, pairs))).start())
            rc(half.at[p], half.at[p], ch + 1, p, p, sib).start()

    def take(half, ch, s, k):
        @pl.when(active & (s > 0))
        def _():
            rc(half.at[k], half.at[k], ch, k, k, sib).wait_recv()
            rc(half.at[k], half.at[k], ch + 1, k, k, sib).start()

        @pl.when(idle)
        def _():
            rc(half.at[k], half.at[k], ch + 1, k, k, sib).wait_recv()

    tile = min(512, points_hbm.shape[0])

    def gram_block(b):
        rows = pl.ds(pl.multiple_of(b * own, own), own)
        block = centers_v[rows, :]
        wide = block.astype(f32)
        centers_aug[:dims, :] = wide.T.astype(bf16)
        centers_aug[dims:, :] = norm_columns(wide, 3, 0).T.astype(bf16)
        for i in range(points_hbm.shape[0] // tile):
            at = slice(i * tile, (i + 1) * tile)
            gram[b, at, :] = exponential(mm(points_aug[at, :], centers_aug[...]))

    points_in.wait()
    for i in range(points_hbm.shape[0] // tile):
        at = slice(i * tile, (i + 1) * tile)
        block = points_v[at, :]
        wide = block.astype(f32)
        points_aug[at, :dims] = (wide * (8.0 / dims)).astype(bf16)
        points_aug[at, dims:] = norm_columns(wide, 0, 3).astype(bf16)
    centers_in.wait()

    unit = n // 16
    marks = [0, unit, 6 * unit, 8 * unit, 13 * unit, 15 * unit, n]

    def gram_blocks(place):
        loop(marks[place], marks[place + 1], gram_block)

    gram_blocks(0)
    pl.semaphore_wait(barrier, 2 * n - 1 + groups // 2 - 1)
    spread(half1, A1)

    acc[...] = jnp.zeros_like(acc)

    def inner_step(s):
        k = back(s)
        take(half1, A1, s, k)
        slab(inner_hbm, inner_v, 0, k).wait()
        acc[...] += nt(half1[k], inner_v[k])

        @pl.when(s < marks[2] - marks[1])
        def _():
            gram_block(marks[1] + s)

    loop(0, pairs, inner_step)

    @pl.when(idle)
    def _():
        ytx1[...] = acc[...]
        single(ytx1, yrx1, Y1).start()

    gram_blocks(2)

    @pl.when(active)
    def _():
        single(ytx1, yrx1, Y1).wait_recv()
        total = acc[...] + yrx1[...]
        inner_term[...] = total
        half2[p] = total.astype(bf16)

    spread(half2, A2)
    acc[...] = jnp.zeros_like(acc)

    def outer_step(s):
        k = back(s)
        take(half2, A2, s, k)
        slab(outer_hbm, outer_v, 1, k).wait()
        acc[...] += nt(half2[k], outer_v[k])

        @pl.when(s < marks[4] - marks[3])
        def _():
            gram_block(marks[3] + s)

    loop(0, pairs, outer_step)

    @pl.when(idle)
    def _():
        ytx2[...] = acc[...]
        single(ytx2, yrx2, Y2).start()

    gram_blocks(4)

    @pl.when(active)
    def _():
        single(ytx2, yrx2, Y2).wait_recv()
        own3[p] = (acc[...] + yrx2[...]).astype(bf16)
        rc(own3.at[p], oth3.at[p], A3Y, p, p, across).start()

    spread(own3, A3)
    gram_blocks(5)
    fit[...] = jnp.zeros_like(fit)

    def fit_step(s):
        k, k1, k2 = back(s), back(s - 1), back(s - 2)

        @pl.when(s < pairs)
        def _():
            take(own3, A3, s, k)

            @pl.when(active & (s > 0))
            def _():
                rc(own3.at[k], oth3.at[k], A3Y, k, k, across).start()

        @pl.when(idle & (s > 0) & (s <= pairs))
        def _():
            rc(oth3.at[k1], oth3.at[k1], A3Y, k1, k1, across).wait_recv()
            rc(oth3.at[k1], oth3.at[k1], A3O, k1, k1, sib).start()

        @pl.when(s < pairs)
        def _():
            fit[...] += nt(own3[k], gram[2 * k + q])

        @pl.when(s >= 2)
        def _():
            @pl.when(active)
            def _():
                rc(oth3.at[k2], oth3.at[k2], A3O, k2, k2, sib).wait_recv()

            fit[...] += nt(oth3[k2], gram[2 * k2 + 1 - q])

    loop(0, pairs + 2, fit_step)
    fit_half[...] = fit[...].astype(bf16)

    def normal_step(s):
        k, k1, k2 = ahead(s), ahead(s - 1 + pairs), ahead(s - 2 + pairs)

        @pl.when(s < pairs)
        def _():
            ctx[k] = mm(fit_half[...], gram[2 * k + 1 - c]).astype(bf16)
            rc(ctx.at[k], nc_rx.at[k], NC, k, k, sib).start()
            keep[k] = mm(fit_half[...], gram[2 * k + c])

        @pl.when((s >= 1) & (s <= pairs))
        def _():
            rc(ctx.at[k1], nc_rx.at[k1], NC, k1, k1, sib).wait_recv()
            total = keep[k1] + nc_rx[k1].astype(f32)

            @pl.when(idle)
            def _():
                ys[k1] = total.astype(bf16)
                rc(ys.at[k1], ny_rx.at[k1], NY, k1, k1, across).start()

            @pl.when(active)
            def _():
                keep[k1] = total

        @pl.when(active & (s >= 2))
        def _():
            rc(ys.at[k2], ny_rx.at[k2], NY, k2, k2, across).wait_recv()
            deliver(keep[k2] + ny_rx[k2].astype(f32), k2, np_rx, NP)

    def deliver(total, k, rx, ch):
        @pl.when(k != p)
        def _():
            tx[k] = total.astype(bf16)
            rc(tx.at[k], rx.at[p], ch, k, p, peer(k)).start()

        @pl.when(k == p)
        def _():
            keep[k] = total

    def collect(rx, ch):
        acc[...] = keep[p]

        def one(s):
            k = back(s)
            rc(tx.at[k], rx.at[k], ch, k, k, sib).wait_recv()
            acc[...] += rx[k].astype(f32)

        loop(1, pairs, one)

    def sent(src, ch, with_own):
        def one(k):
            if with_own:
                rc(src.at[k], src.at[k], ch, k, k, sib).wait_send()
            else:
                @pl.when(k != p)
                def _():
                    rc(src.at[k], src.at[k], ch, k, k, sib).wait_send()
        loop(0, pairs, one)

    loop(0, pairs + 2, normal_step)
    sent(ctx, NC, True)

    @pl.when(active)
    def _():
        collect(np_rx, NP)
        if groups > 2:
            mine = g // 2
            pair_sums[mine] = acc[...]

            def pair_copy(h, to):
                return pltpu.make_async_remote_copy(
                    src_ref=pair_sums.at[h], dst_ref=pair_sums.at[h], send_sem=psend.at[to],
                    recv_sem=precv.at[h], device_id=(2 * to + q, r), device_id_type=MESH)

            for h in range(groups // 2):
                @pl.when(h != mine)
                def _():
                    pair_copy(mine, h).start()
            for h in range(groups // 2):
                @pl.when(h != mine)
                def _():
                    pair_copy(h, h).wait_recv()
            total = pair_sums[0]
            for h in range(1, groups // 2):
                total = total + pair_sums[h]
            acc[...] = total
            for h in range(groups // 2):
                @pl.when(h != mine)
                def _():
                    pair_copy(mine, h).wait_send()
        normal_half[...] = acc[...].astype(bf16)
        single(normal_half, normal_half, YN).start()
        sent(tx, NP, False)

    @pl.when(idle)
    def _():
        single(normal_half, normal_half, YN).wait_recv()

    def transposed(held, lhs, s_rx, p_rx, ch_s, ch_p):
        def one(s):
            k, k1 = ahead(s), ahead(s - 1 + pairs)

            @pl.when(s < pairs)
            def _():
                term = mm(lhs[...], held[k])

                @pl.when(idle)
                def _():
                    ctx[k] = term.astype(bf16)
                    rc(ctx.at[k], s_rx.at[k], ch_s, k, k, sib).start()

                @pl.when(active)
                def _():
                    keep[k] = term

            @pl.when(active & (s >= 1))
            def _():
                rc(ctx.at[k1], s_rx.at[k1], ch_s, k1, k1, sib).wait_recv()
                deliver(keep[k1] + s_rx[k1].astype(f32), k1, p_rx, ch_p)

        loop(0, pairs + 1, one)

        @pl.when(active)
        def _():
            collect(p_rx, ch_p)
            sent(tx, ch_p, False)

        @pl.when(idle)
        def _():
            sent(ctx, ch_s, True)

    transposed(outer_v, normal_half, os_rx, op_rx, O_S, O_P)

    @pl.when(active)
    def _():
        shaped = acc[...] * (1.0 / point_count) + ridge_weight * inner_term[...]
        shaped_half[...] = shaped.astype(bf16)
        single(shaped_half, shaped_half, YS).start()

    @pl.when(idle)
    def _():
        single(shaped_half, shaped_half, YS).wait_recv()

    transposed(inner_v, shaped_half, is_rx, ip_rx, I_S, I_P)

    def dot_copy(slot, d):
        return pltpu.make_async_remote_copy(
            src_ref=dots.at[slot], dst_ref=dots.at[slot], send_sem=dsend.at[d], recv_sem=drecv.at[slot],
            device_id=(base + d // n, lax.rem(d, n)), device_id_type=MESH)

    me = q * n + r
    lane = lax.broadcasted_iota(jnp.int32, (targets, 128), 1)

    @pl.when(active)
    def _():
        image[...] = acc[...]
        x, y, z = acc[...], residual[...], direction[...]
        packed = jnp.zeros((targets, 128), f32)
        for at, pair in enumerate(((y, y), (z, x), (y, x), (x, x))):
            packed = jnp.where(lane == at, jnp.sum(pair[0] * pair[1], axis=1, keepdims=True), packed)
        square = jnp.concatenate([packed, jnp.zeros((128 - targets, 128), f32)], axis=0)
        dots[r] = square.T[:8, :]

        def one(d):
            @pl.when(d != me)
            def _():
                dot_copy(r, d).start()

        loop(0, 2 * n, one)
        single(image, image, YI).start()

    def arrived(slot):
        @pl.when(idle | (slot != r))
        def _():
            dot_copy(slot, me).wait_recv()

    loop(0, n, arrived)
    totals = dots[0]
    for slot in range(1, n):
        totals = totals + dots[slot]
    square = jnp.concatenate([totals, jnp.zeros((120, 128), f32)], axis=0).T

    @pl.when(idle)
    def _():
        single(image, image, YI).wait_recv()

    old_norm, curvature = square[:targets, 0:1], square[:targets, 1:2]
    cross_sum, image_norm = square[:targets, 2:3], square[:targets, 3:4]
    step_size = old_norm / curvature
    new_norm = old_norm - 2.0 * step_size * cross_sum + step_size * step_size * image_norm
    factors[...] = jnp.where(lane == 0, step_size, new_norm / old_norm)

    @pl.when(active)
    def _():
        sent(half1, A1, False)
        sent(half1, A1S, True)
        sent(half2, A2, False)
        sent(half2, A2S, True)
        sent(own3, A3, False)
        sent(own3, A3S, True)
        sent(own3, A3Y, True)
        single(normal_half, normal_half, YN).wait_send()
        single(shaped_half, shaped_half, YS).wait_send()
        single(image, image, YI).wait_send()

        def one(d):
            @pl.when(d != me)
            def _():
                dot_copy(r, d).wait_send()

        loop(0, 2 * n, one)

    @pl.when(idle)
    def _():
        single(ytx1, yrx1, Y1).wait_send()
        single(ytx2, yrx2, Y2).wait_send()
        sent(oth3, A3O, True)
        sent(ys, NY, True)


def update(image, factors, iterate, residual, direction, next_iterate, next_residual, next_direction):
    step_size, ratio = factors[:, 0:1], factors[:, 1:2]
    following = residual[...] - step_size * image[...]
    next_residual[...] = following
    next_iterate[...] = iterate[...] + step_size * direction[...]
    next_direction[...] = following + ratio * direction[...]


def local(groups, n, points, centers, inner_factor, outer_factor, iterate, residual, direction):
    pairs, own = n // 2, inner_factor.shape[0]
    count, dims = points.shape
    targets = direction.shape[0]
    half = pltpu.VMEM((pairs, targets, own), bf16)
    block = pltpu.VMEM((targets, own), f32)
    slabs = pltpu.VMEM((pairs, own, own), bf16)
    vmem = pl.BlockSpec(memory_space=pltpu.VMEM)
    anywhere = pl.BlockSpec(memory_space=pl.ANY)
    dma = pltpu.SemaphoreType.DMA
    image, factors = pl.pallas_call(
        functools.partial(kernel, groups, n, count * groups * n),
        out_shape=[jax.ShapeDtypeStruct((targets, own), f32), jax.ShapeDtypeStruct((targets, 128), f32)],
        in_specs=[anywhere] * 4 + [vmem] * 2,
        out_specs=[vmem] * 2,
        scratch_shapes=[
            pltpu.VMEM((n, count, own), bf16), slabs, slabs,
            pltpu.VMEM((count, dims), bf16), pltpu.VMEM(centers.shape, bf16),
            pltpu.VMEM((count, 2 * dims), bf16), pltpu.VMEM((2 * dims, own), bf16),
            half, half, half, half,
            pltpu.VMEM((targets, count), f32), pltpu.VMEM((targets, count), bf16),
            block, block, block, block, block, block,
            half, pltpu.VMEM((pairs, targets, own), f32), half, half,
            half, half, half, half, half, half, half,
            pltpu.VMEM((targets, own), bf16), pltpu.VMEM((targets, own), bf16),
            pltpu.VMEM((max(groups // 2, 1), targets, own) if groups > 2 else (1, 8, 128), f32),
            pltpu.VMEM((n, 8, 128), f32),
            dma((3, max(pairs, 2))), dma((CHANNELS, pairs)), dma((CHANNELS, pairs)),
            dma((SINGLES,)), dma((SINGLES,)),
            dma((max(groups // 2, 1),)), dma((max(groups // 2, 1),)), dma((2 * n,)), dma((n,)),
        ],
        compiler_params=pltpu.CompilerParams(
            collective_id=0, has_side_effects=True, vmem_limit_bytes=60 * 1024 * 1024
        ),
        cost_estimate=pl.CostEstimate(
            flops=2 * count * centers.shape[0] * (dims + 2 * targets),
            bytes_accessed=4 * own * centers.shape[0], transcendentals=count * centers.shape[0]),
    )(points, centers, inner_factor, outer_factor, residual, direction)
    return tuple(pl.pallas_call(
        update,
        out_shape=[jax.ShapeDtypeStruct((targets, own), f32)] * 3,
        in_specs=[vmem] * 5,
        out_specs=[vmem] * 3,
    )(image, factors, iterate, residual, direction))


def solution(mesh):
    placed = (
        P(("grp", "row"), None), P(), P("row", None), P("row", None),
        P(None, "row"), P(None, "row"), P(None, "row"),
    )
    return jax.shard_map(
        functools.partial(local, mesh.shape["grp"], mesh.shape["row"]),
        mesh=mesh,
        in_specs=placed,
        out_specs=(P(None, "row"), P(None, "row"), P(None, "row")),
        check_vma=False,
    )
```
